768 devices in a mesh: band: 12 (over z), feat: 64 (over x, y, core).
Axes of the slice: x: 4, y: 8, z: 12, core: 2. Of those that a mesh axis runs over, the one named last changes fastest.
Arguments:
- grid_latent: bfloat16 [196608, 512], P(('band', 'feat')), may hold values from -6 to 6
- mesh_latent: bfloat16 [6144, 512], P(('band', 'feat')), may hold values from -6 to 6
- g2m_src: int32 [393216], P(('band', 'feat')), may hold values from 0 to 255
- g2m_peer: int32 [393216, 1], P(('band', 'feat')), may hold values from 0 to 63; in each aligned block of 512 rows (0 to 511, 512 to 1023, ...) at most 16 rows name the same one
- g2m_slot: int32 [393216], P(('band', 'feat')), may hold values from 0 to 7
- proc_src: int32 [196608], P(('band', 'feat')), may hold values from 0 to 23
- proc_dst: int32 [196608], P(('band', 'feat')), may hold values from 0 to 7
- enc_src_w: bfloat16 [512, 512], replicated, may hold values from -0.25 to 0.25
- enc_dst_w: bfloat16 [512, 512], replicated, may hold values from -0.25 to 0.25
- enc_out_w: bfloat16 [512, 512], replicated, may hold values from -0.25 to 0.25
- enc_bias: float32 [512], replicated, may hold values from -3 to 3
- enc_gain: float32 [512], replicated, may hold values from 0.25 to 1.75
- proc_src_w: bfloat16 [512, 512], replicated, may hold values from -0.25 to 0.25
- proc_dst_w: bfloat16 [512, 512], replicated, may hold values from -0.25 to 0.25
- proc_out_w: bfloat16 [512, 512], replicated, may hold values from -0.25 to 0.25
- proc_bias: float32 [512], replicated, may hold values from -3 to 3
- proc_gain: float32 [512], replicated, may hold values from 0.25 to 1.75
- cotangent: bfloat16 [6144, 512], P(('band', 'feat')), may hold values from -6 to 6
Outputs:
- mesh_out: bfloat16 [6144, 512], P(('band', 'feat'))
- grad_grid: bfloat16 [196608, 512], P(('band', 'feat'))
- grad_mesh: bfloat16 [6144, 512], P(('band', 'feat'))
The draws below stay inside these ranges and needn't reach their ends.
Inputs may be any that keep to these rules, and one draw needn't show every extreme that they name: `g2m_peer`: among the edges of one device at most 16 name the same peer, a bound that some block reaches.
All inputs are finite; a program needn't handle non-finite values.
Results may differ from the reference program's by a relative error of at most 0.015.
Values may be sent and summed in bfloat16 or wider, within the bound.
No kernel may reach another device: no remote copies, remote signals or barrier semaphores. Data moves between devices by JAX's collectives and lax.ppermute only.
A program may use at most 32 MiB of HBM per device.

```python
import math
import jax
import jax.numpy as jnp
import numpy as np
from jax import lax

C = 512
GRID_DEV = 256
MESH_DEV = 8
E_DEV = 512
P_DEV = 256
CAP = 16
GRID = 196608
MESH = 6144
EDGES = 393216
PEDGES = 196608
N_BAND = 12
N_FEAT = 64


def set_ends(values, key, smallest, top_value):
    longest = values.shape.index(max(values.shape))
    spots = []
    for shift in (0, 1):
        where = [jax.random.randint(jax.random.fold_in(key, axis), (), 0, length) for axis, length in enumerate(values.shape)]
        where[longest] = (where[longest] + shift) % values.shape[longest]
        spots.append(tuple(where))
    return values.at[spots[0]].set(smallest).at[spots[1]].set(top_value)


def levels(stream_key, dims, pieces, low, largest):
    level, own = 1.0, jax.random.fold_in(stream_key, 6)
    for axis_at, shards_of in pieces:
        steps = jnp.exp(jax.random.uniform(jax.random.fold_in(own, axis_at), (shards_of,), jnp.float32, low / len(pieces), largest / len(pieces)))
        level = level * jnp.repeat(steps, dims[axis_at] // shards_of).reshape([-1 if axis == axis_at else 1 for axis in range(len(dims))])
    return level


def shared_out(stream_key, own, number, rows, amount, top, reach, lean):
    ranking = jax.random.permutation(stream_key, amount)
    crowded, ordinary = load_shares(amount, rows * top, reach, lean, True), load_shares(amount, rows * top, reach, lean, False)
    places = jnp.arange(amount)

    def named(sizes, turn):
        used = int((sizes > 0).sum())
        fixed = max(1, used // 4)
        passed = fixed + (places - fixed + turn * (used - fixed)) % max(1, amount - fixed)
        return jnp.zeros((amount,), jnp.int32).at[ranking[jnp.where(places < fixed, places, passed)]].set(jnp.asarray(sizes, jnp.int32))

    sizes = jnp.where(number % 4 == 0, named(crowded, number // 4), named(ordinary, number - number // 4 - 1))
    mixed = jax.random.permutation(jax.random.fold_in(own, 3), amount)
    source_of, receiver = mixed[0:amount // 2 * 2:2], mixed[1:amount // 2 * 2:2]
    slack = jnp.minimum(sizes[source_of] - 1, reach - sizes[receiver]) // 2
    slack = jnp.where((source_of == ranking[0]) | (receiver == ranking[0]) | (sizes[receiver] == 0), 0, jnp.maximum(slack, 0))
    passed = jax.random.randint(jax.random.fold_in(own, 4), (amount // 2,), 0, 1 << 20) % (slack + 1)
    sizes = sizes.at[source_of].add(-passed).at[receiver].add(passed)
    members = jnp.searchsorted(jnp.cumsum(sizes), jnp.arange(rows * top), side="right").astype(jnp.int32)
    grid = members.reshape(top, rows).T
    grid = grid[jax.random.permutation(jax.random.fold_in(own, 1), rows)]
    turn = jax.random.randint(jax.random.fold_in(own, 2), (rows, 1), 0, top)
    return jnp.take_along_axis(grid, (jnp.arange(top)[None, :] + turn) % top, axis=1)


def load_shares(amount, total, limit, slope, full):
    loads = [(1 << 20) // math.isqrt(grade ** slope) + 1 for grade in range(1, amount + 1)]
    largest = limit if full else min(limit, max(-(-total // amount), total * loads[0] // sum(loads)))
    least = 1 if total - largest >= amount - 1 else 0
    counts, spare = [largest] + [least] * (amount - 1), total - largest - least * (amount - 1)
    while spare > 0:
        candidates = [i for i in range(1, amount) if counts[i] < largest] or [i for i in range(1, amount) if counts[i] < limit]
        pool, budget = sum([loads[i] for i in candidates]), spare
        for i in candidates:
            extra = min(limit - counts[i], max(1, budget * loads[i] // pool), spare)
            counts[i] = counts[i] + extra
            spare = spare - extra
    return np.array(counts)


def bell_draw(rng, shape, deviation, reach, pieces=(), kind=jnp.bfloat16):
    values = jax.random.normal(rng, shape, jnp.float32) * deviation
    if len(pieces) > 0:
        values = levels(rng, shape, pieces, -0.22, 0.18) * values
    return jnp.clip(values, min=-reach, max=reach).astype(kind)


def setup_inputs(seed: int = 0) -> dict:
    seeds = jax.random.split(jax.random.key(seed), 19)
    grid_latent = bell_draw(seeds[0], (GRID, C), 1.0, 6.0, ((0, 768),))
    mesh_latent = bell_draw(seeds[1], (MESH, C), 1.0, 6.0, ((0, 768),))
    g2m_src = set_ends(jax.random.randint(seeds[2], (EDGES,), 0, GRID_DEV), jax.random.fold_in(seeds[2], 1), 0, GRID_DEV - 1).astype(jnp.int32)
    g2m_peer_keys = jax.random.split(jax.random.fold_in(seeds[3], 1), EDGES // E_DEV)
    g2m_peer_turns = jax.random.permutation(jax.random.fold_in(seeds[3], 3), EDGES // E_DEV)
    g2m_peer = jax.vmap(lambda own, number: shared_out(jax.random.fold_in(seeds[3], 2), own, number, E_DEV, N_FEAT, 1, CAP, 2))(g2m_peer_keys, g2m_peer_turns).reshape((EDGES, 1))
    g2m_slot = set_ends(jax.random.randint(seeds[4], (EDGES,), 0, MESH_DEV), jax.random.fold_in(seeds[4], 1), 0, MESH_DEV - 1).astype(jnp.int32)
    proc_src = set_ends(jax.random.randint(seeds[5], (PEDGES,), 0, 3 * MESH_DEV), jax.random.fold_in(seeds[5], 1), 0, (3 * MESH_DEV) - 1).astype(jnp.int32)
    proc_dst = set_ends(jax.random.randint(seeds[6], (PEDGES,), 0, MESH_DEV), jax.random.fold_in(seeds[6], 1), 0, MESH_DEV - 1).astype(jnp.int32)
    enc_src_w = bell_draw(seeds[7], (C, C), C ** -0.5, 0.25)
    enc_dst_w = bell_draw(seeds[8], (C, C), C ** -0.5, 0.25)
    enc_out_w = bell_draw(seeds[9], (C, C), C ** -0.5, 0.25)
    enc_bias = bell_draw(seeds[10], (C,), 0.5, 3.0, (), jnp.float32)
    enc_gain = jnp.clip(1.0 + 0.15 * jax.random.normal(seeds[11], (C,), jnp.float32), 0.25, 1.75)
    proc_src_w = bell_draw(seeds[12], (C, C), C ** -0.5, 0.25)
    proc_dst_w = bell_draw(seeds[13], (C, C), C ** -0.5, 0.25)
    proc_out_w = bell_draw(seeds[14], (C, C), C ** -0.5, 0.25)
    proc_bias = bell_draw(seeds[15], (C,), 0.5, 3.0, (), jnp.float32)
    proc_gain = jnp.clip(1.0 + 0.15 * jax.random.normal(seeds[16], (C,), jnp.float32), 0.25, 1.75)
    cotangent = bell_draw(seeds[17], (MESH, C), 1.0, 6.0, ((0, 768),))
    return {"grid_latent": grid_latent, "mesh_latent": mesh_latent, "g2m_src": g2m_src, "g2m_peer": g2m_peer, "g2m_slot": g2m_slot, "proc_src": proc_src, "proc_dst": proc_dst, "enc_src_w": enc_src_w, "enc_dst_w": enc_dst_w, "enc_out_w": enc_out_w, "enc_bias": enc_bias, "enc_gain": enc_gain, "proc_src_w": proc_src_w, "proc_dst_w": proc_dst_w, "proc_out_w": proc_out_w, "proc_bias": proc_bias, "proc_gain": proc_gain, "cotangent": cotangent}


def layer_norm(values, gain):
    average = lax.optimization_barrier(jnp.mean(values, axis=-1, keepdims=True))
    centred = values - average
    spread = lax.optimization_barrier(jnp.mean(centred * centred, axis=-1, keepdims=True))
    inv_std = lax.rsqrt(spread + 1e-05)
    normed = centred * inv_std
    return (normed * gain, normed, inv_std)

def norm_back(normed, inv_std, gain, upstream):
    scaled = upstream * gain
    return inv_std * (scaled - lax.optimization_barrier(jnp.mean(scaled, axis=-1, keepdims=True)) - normed * lax.optimization_barrier(jnp.mean(scaled * normed, axis=-1, keepdims=True)))

def silu_grad(values):
    sigma = jax.nn.sigmoid(values)
    return sigma * (1.0 + values * (1.0 - sigma))

def times_transpose(left, weight):
    return lax.dot_general(left, weight, (((1,), (1,)), ((), ())), preferred_element_type=jnp.float32)

def reference(grid_latent, mesh_latent, g2m_src, g2m_peer, g2m_slot, proc_src, proc_dst, enc_src_w, enc_dst_w, enc_out_w, enc_bias, enc_gain, proc_src_w, proc_dst_w, proc_out_w, proc_bias, proc_gain, cotangent):
    edge_device = jnp.arange(EDGES, dtype=jnp.int32) // E_DEV
    grid_idx = (edge_device * GRID_DEV + g2m_src).astype(jnp.int32)
    mesh_idx = ((edge_device // N_FEAT * N_FEAT + g2m_peer[:, 0]) * MESH_DEV + g2m_slot).astype(jnp.int32)
    dst_proj = jnp.dot(mesh_latent, enc_dst_w, preferred_element_type=jnp.float32)
    enc_pre = jnp.dot(grid_latent[grid_idx], enc_src_w, preferred_element_type=jnp.float32) + dst_proj[mesh_idx] + enc_bias
    enc_hid = jax.nn.silu(enc_pre).astype(jnp.bfloat16)
    enc_msg = jnp.dot(enc_hid, enc_out_w, preferred_element_type=jnp.float32)
    enc_agg = jax.ops.segment_sum(enc_msg, mesh_idx, num_segments=MESH)
    enc_norm, enc_hat, enc_inv = layer_norm(enc_agg, enc_gain)
    mesh_mid = (mesh_latent.astype(jnp.float32) + enc_norm).astype(jnp.bfloat16)
    proc_device = jnp.arange(PEDGES, dtype=jnp.int32) // P_DEV
    proc_band = proc_device // N_FEAT
    offset = proc_src // MESH_DEV - 1
    inside = jnp.logical_and(proc_band + offset >= 0, proc_band + offset < N_BAND)
    src_idx = jnp.clip((proc_device + offset * N_FEAT) * MESH_DEV + proc_src % MESH_DEV, 0, MESH - 1).astype(jnp.int32)
    dst_idx = (proc_device * MESH_DEV + proc_dst).astype(jnp.int32)
    src_rows = jnp.where(inside[:, None], mesh_mid[src_idx], jnp.zeros((), mesh_mid.dtype))
    pdst_proj = jnp.dot(mesh_mid, proc_dst_w, preferred_element_type=jnp.float32)
    proc_pre = jnp.dot(src_rows, proc_src_w, preferred_element_type=jnp.float32) + pdst_proj[dst_idx] + proc_bias
    proc_hid = jax.nn.silu(proc_pre).astype(jnp.bfloat16)
    proc_msg = jnp.dot(proc_hid, proc_out_w, preferred_element_type=jnp.float32)
    proc_agg = jax.ops.segment_sum(proc_msg, dst_idx, num_segments=MESH)
    proc_norm, proc_hat, proc_inv = layer_norm(proc_agg, proc_gain)
    mesh_out = (mesh_mid.astype(jnp.float32) + proc_norm).astype(jnp.bfloat16)
    upstream = cotangent.astype(jnp.float32)
    grad_proc_agg = norm_back(proc_hat, proc_inv, proc_gain, upstream)
    proc_msg_grad = grad_proc_agg[dst_idx].astype(jnp.bfloat16)
    proc_pre_grad = (times_transpose(proc_msg_grad, proc_out_w) * silu_grad(proc_pre)).astype(jnp.bfloat16)
    sender_grad = times_transpose(proc_pre_grad, proc_src_w) * inside[:, None].astype(jnp.float32)
    receiver_grad = times_transpose(proc_pre_grad, proc_dst_w)
    grad_mid = upstream + jax.ops.segment_sum(receiver_grad, dst_idx, num_segments=MESH) + jax.ops.segment_sum(sender_grad, src_idx, num_segments=MESH)
    grad_enc_agg = norm_back(enc_hat, enc_inv, enc_gain, grad_mid)
    enc_msg_grad = grad_enc_agg[mesh_idx].astype(jnp.bfloat16)
    enc_pre_grad = (times_transpose(enc_msg_grad, enc_out_w) * silu_grad(enc_pre)).astype(jnp.bfloat16)
    row_grad = times_transpose(enc_pre_grad, enc_src_w)
    grad_grid = jax.ops.segment_sum(row_grad, grid_idx, num_segments=GRID).astype(jnp.bfloat16)
    node_grad = times_transpose(enc_pre_grad, enc_dst_w)
    grad_mesh = (grad_mid + jax.ops.segment_sum(node_grad, mesh_idx, num_segments=MESH)).astype(jnp.bfloat16)
    return (mesh_out, grad_grid, grad_mesh)
```

```python
import functools

import jax
import jax.numpy as jnp
from jax import lax
from jax.experimental import pallas as pl
from jax.experimental.pallas import tpu as pltpu
from jax.sharding import PartitionSpec as P

BF16 = jnp.bfloat16
F32 = jnp.float32


def dot(left, right):
    return jnp.dot(left, right, preferred_element_type=F32)


def dot_t(left, right):
    return lax.dot_general(left, right, (((1,), (1,)), ((), ())), preferred_element_type=F32)


def split(values):
    high = values.astype(BF16)
    return high, (values - high.astype(F32)).astype(BF16)


def wide_dot(values, weight, product):
    rows = values.shape[0]
    high, low = split(values)
    both = product(jnp.concatenate([high.astype(F32), low.astype(F32)], axis=0).astype(BF16), weight)
    return both[:rows] + both[rows:]


def thirds(values):
    high, rest = values.astype(BF16), values
    rest = rest - high.astype(F32)
    mid = rest.astype(BF16).astype(F32)
    low = (rest - mid).astype(BF16).astype(F32)
    return jnp.concatenate([high.astype(F32), mid, low], axis=0).astype(BF16)


def layer_norm(values, gain):
    average = jnp.mean(values, axis=-1, keepdims=True)
    centred = values - average
    spread = jnp.mean(centred * centred, axis=-1, keepdims=True)
    inv_std = lax.rsqrt(spread + 1e-05)
    normed = centred * inv_std
    return normed * gain, normed, inv_std


def norm_back(normed, inv_std, gain, upstream):
    scaled = upstream * gain
    return inv_std * (
        scaled
        - jnp.mean(scaled, axis=-1, keepdims=True)
        - normed * jnp.mean(scaled * normed, axis=-1, keepdims=True)
    )


def call(body, out, *args, scratch=()):
    flops = 4e9
    return pl.pallas_call(
        body,
        out_shape=out,
        in_specs=[pl.BlockSpec(memory_space=pltpu.VMEM)] * len(args),
        out_specs=jax.tree.map(lambda _: pl.BlockSpec(memory_space=pltpu.VMEM), out),
        scratch_shapes=scratch,
        compiler_params=pltpu.CompilerParams(vmem_limit_bytes=40 * 2**20),
        cost_estimate=pl.CostEstimate(flops=int(flops), bytes_accessed=2**22, transcendentals=0),
    )(*args)


def src_kernel(own_ref, mate_ref, pick_ref, weight_ref, bias_ref, pre_ref):
    tile = own_ref.shape[0]
    edges = pick_ref.shape[0]
    for start in range(0, edges, tile):
        grid_ref = own_ref if start < edges // 2 else mate_ref
        rows = dot(pick_ref[start : start + tile, :], grid_ref[...]).astype(BF16)
        pre_ref[start : start + tile, :] = dot(rows, weight_ref[...]) + bias_ref[...]


def enc_kernel(pre_ref, dst_ref, dst_t_ref, mesh_ref, weight_ref, sum_ref, slope_ref):
    tile = 256
    total = None
    for start in range(0, pre_ref.shape[0], tile):
        rows = dot(dst_ref[start : start + tile, :], mesh_ref[...]).astype(BF16)
        pre = pre_ref[start : start + tile, :] + dot(rows, weight_ref[...])
        sigma = jax.nn.sigmoid(pre)
        hidden = (pre * sigma).astype(BF16)
        slope_ref[start : start + tile, :] = sigma * (1.0 + pre * (1.0 - sigma))
        part = dot(dst_t_ref[:, start : start + tile], hidden)
        total = part if total is None else total + part
    sum_ref[...] = total.astype(BF16)


def chunk_sum(ref, count):
    values = ref[...].astype(F32)
    return jnp.sum(values.reshape(values.shape[0] // count, count, values.shape[1]), axis=0)


def mid_kernel(parts_ref, weight_ref, gain_ref, mesh_ref, mid_ref, agg_ref):
    agg = wide_dot(chunk_sum(parts_ref, mesh_ref.shape[0]), weight_ref[...], dot)
    agg_ref[...] = agg
    mid_ref[...] = (mesh_ref[...].astype(F32) + layer_norm(agg, gain_ref[...])[0]).astype(BF16)


def proc_kernel(
    one_ref, mid_ref, two_ref, pick_ref, pick_t_ref, src_w_ref, dst_w_ref, out_w_ref, bias_ref,
    gain_ref, cotangent_ref, out_ref, rim_one_ref, rim_two_ref, grad_ref,
):
    count = mid_ref.shape[0]
    mid = mid_ref[...].astype(F32)
    near = jnp.concatenate([one_ref[...].astype(F32), mid, two_ref[...].astype(F32)], axis=0)
    table = jnp.concatenate(
        [dot(near.astype(BF16), src_w_ref[...]), dot(mid.astype(BF16), dst_w_ref[...]) + bias_ref[...]],
        axis=0,
    )
    pre = dot(pick_ref[...], thirds(table))
    sigma = jax.nn.sigmoid(pre)
    hidden = (pre * sigma).astype(BF16)
    slope = sigma * (1.0 + pre * (1.0 - sigma))
    summed = dot(pick_t_ref[...], hidden)[3 * count :]
    agg = wide_dot(summed, out_w_ref[...], dot)
    shifted, normed, inv_std = layer_norm(agg, gain_ref[...])
    out_ref[...] = (mid + shifted).astype(BF16)
    upstream = cotangent_ref[...].astype(F32)
    grad_agg = norm_back(normed, inv_std, gain_ref[...], upstream).astype(BF16)
    back = dot_t(grad_agg, out_w_ref[...])
    blank = jnp.zeros((3 * count, back.shape[1]), F32)
    spread = dot(pick_ref[...], thirds(jnp.concatenate([blank, back], axis=0)))
    pre_grad = (spread * slope).astype(BF16)
    sums = dot(pick_t_ref[...], pre_grad)
    sender = wide_dot(sums[: 3 * count], src_w_ref[...], dot_t)
    receiver = wide_dot(sums[3 * count :], dst_w_ref[...], dot_t)
    rim_one_ref[...] = sender[:count].astype(BF16)
    rim_two_ref[...] = sender[2 * count :].astype(BF16)
    grad_ref[...] = upstream + receiver + sender[count : 2 * count]


def back_kernel(part_ref, one_ref, two_ref, agg_ref, gain_ref, grad_ref, tiled_ref):
    grad = part_ref[...] + one_ref[...].astype(F32) + two_ref[...].astype(F32)
    grad_ref[...] = grad
    _, normed, inv_std = layer_norm(agg_ref[...], gain_ref[...])
    rows = norm_back(normed, inv_std, gain_ref[...], grad)
    times = tiled_ref.shape[0] // rows.shape[0]
    tiled_ref[...] = jnp.concatenate([rows] * times, axis=0).astype(BF16)


def enc_back_kernel(grad_ref, dst_ref, dst_t_ref, slope_ref, weight_ref, edge_ref, sum_ref):
    tile = 256
    total = None
    for start in range(0, slope_ref.shape[0], tile):
        rows = dot(dst_ref[start : start + tile, :], grad_ref[...]).astype(BF16)
        edge = (dot_t(rows, weight_ref[...]) * slope_ref[start : start + tile, :]).astype(BF16)
        edge_ref[start : start + tile, :] = edge
        part = dot(dst_t_ref[:, start : start + tile], edge)
        total = part if total is None else total + part
    sum_ref[...] = total.astype(BF16)


def grid_kernel(edge_ref, pick_t_ref, weight_ref, own_ref, mate_ref):
    half = edge_ref.shape[0] // 2
    own = dot(pick_t_ref[:, :half], edge_ref[:half, :])
    mate = dot(pick_t_ref[:, half:], edge_ref[half:, :])
    own_ref[...] = wide_dot(own, weight_ref[...], dot_t)
    mate_ref[...] = wide_dot(mate, weight_ref[...], dot_t).astype(BF16)


def mesh_kernel(parts_ref, weight_ref, grad_ref, out_ref):
    summed = chunk_sum(parts_ref, grad_ref.shape[0])
    out_ref[...] = (grad_ref[...] + wide_dot(summed, weight_ref[...], dot_t)).astype(BF16)


def per_device(
    grid_latent,
    mesh_latent,
    g2m_src,
    g2m_peer,
    g2m_slot,
    proc_src,
    proc_dst,
    enc_src_w,
    enc_dst_w,
    enc_out_w,
    enc_bias,
    enc_gain,
    proc_src_w,
    proc_dst_w,
    proc_out_w,
    proc_bias,
    proc_gain,
    cotangent,
):
    feats = lax.axis_size("feat")
    bands = lax.axis_size("band")
    chips = feats // 2
    core = lax.axis_index("feat") % 2
    band = lax.axis_index("band")
    edges = g2m_src.shape[0]
    grids, latent = grid_latent.shape
    nodes = mesh_latent.shape[0]
    plane_nodes = chips * nodes
    plane = [[2 * chip + side for chip in range(chips)] for side in range(2)]
    shape = jax.ShapeDtypeStruct
    row = lambda vector: vector.reshape(1, latent)

    def exchange(values):
        parts = values.reshape(chips, nodes, latent)
        parts = lax.all_to_all(
            parts, "feat", split_axis=0, concat_axis=0, tiled=True, axis_index_groups=plane
        )
        return parts.reshape(plane_nodes, latent)

    def swap(values):
        return lax.ppermute(values, "feat", [(i, i ^ 1) for i in range(feats)])

    first = [(i, i ^ 1) for i in range(bands)]
    second = [(i, j) for i in range(1, bands - 2, 2) for i, j in ((i, i + 1), (i + 1, i))]

    mesh_all = exchange(jnp.tile(mesh_latent, (chips, 1)))

    mate_grid = swap(grid_latent)
    index = jnp.stack([g2m_src, g2m_peer[:, 0], g2m_slot])
    index = jnp.concatenate([index, swap(index)], axis=1)
    source, peer, slot = index[0], index[1], index[2]
    target = jnp.where(peer % 2 == core, peer // 2 * nodes + slot, -1)
    grid_ids = jnp.arange(grids, dtype=jnp.int32)
    node_ids = jnp.arange(plane_nodes, dtype=jnp.int32)
    src_pick = (source[:, None] == grid_ids[None, :]).astype(BF16)
    src_pick_t = (source[None, :] == grid_ids[:, None]).astype(BF16)
    dst_pick = (target[:, None] == node_ids[None, :]).astype(BF16)
    dst_pick_t = (target[None, :] == node_ids[:, None]).astype(BF16)

    side = proc_src // nodes
    sender = jnp.where(band % 2 == 0, 2 - side, side) * nodes + proc_src % nodes
    table_ids = jnp.arange(4 * nodes, dtype=jnp.int32)

    def proc_pick(ids, per_edge):
        return jnp.logical_or(per_edge(sender) == ids, per_edge(proc_dst + 3 * nodes) == ids).astype(BF16)

    pick = proc_pick(jnp.tile(table_ids, 3)[None, :], lambda v: v[:, None])
    pick_t = proc_pick(table_ids[:, None], lambda v: v[None, :])

    pre_src = call(
        src_kernel, shape((2 * edges, latent), F32),
        grid_latent, mate_grid, src_pick, enc_src_w, row(enc_bias),
    )
    partial, slope = call(
        enc_kernel, (shape((plane_nodes, latent), BF16), shape((2 * edges, latent), F32)),
        pre_src, dst_pick, dst_pick_t, mesh_all, enc_dst_w,
    )
    mid, enc_agg = call(
        mid_kernel, (shape((nodes, latent), BF16), shape((nodes, latent), F32)),
        exchange(partial), enc_out_w, row(enc_gain), mesh_latent,
    )
    one = lax.ppermute(mid, "band", first)
    two = lax.ppermute(mid, "band", second)
    mesh_out, rim_one, rim_two, grad_part = call(
        proc_kernel,
        (shape((nodes, latent), BF16),) * 3 + (shape((nodes, latent), F32),),
        one, mid, two, pick, pick_t, proc_src_w, proc_dst_w, proc_out_w, row(proc_bias),
        row(proc_gain), cotangent,
    )
    back_one = lax.ppermute(rim_one, "band", first)
    back_two = lax.ppermute(rim_two, "band", second)
    grad_mid, tiled = call(
        back_kernel, (shape((nodes, latent), F32), shape((plane_nodes, latent), BF16)),
        grad_part, back_one, back_two, enc_agg, row(enc_gain),
    )
    edge_grad, node_part = call(
        enc_back_kernel, (shape((2 * edges, latent), BF16), shape((plane_nodes, latent), BF16)),
        exchange(tiled), dst_pick, dst_pick_t, slope, enc_out_w,
    )
    node_parts = exchange(node_part)
    own_grad, mate_grad = call(
        grid_kernel, (shape((grids, latent), F32), shape((grids, latent), BF16)),
        edge_grad, src_pick_t, enc_src_w,
    )
    grad_grid = (own_grad + swap(mate_grad).astype(F32)).astype(BF16)
    grad_mesh = call(
        mesh_kernel, shape((nodes, latent), BF16), node_parts, enc_dst_w, grad_mid,
    )
    return (mesh_out, grad_grid, grad_mesh)


def solution(mesh):
    shard = ("band", "feat")
    placed = (P(shard, None), P(shard, None), P(shard), P(shard, None), P(shard), P(shard), P(shard))
    placed += (P(),) * 10 + (P(shard, None),)
    return jax.shard_map(
        per_device,
        mesh=mesh,
        in_specs=placed,
        out_specs=(P(shard, None), P(shard, None), P(shard, None)),
        check_vma=False,
    )
```

```python
import jax
import jax.numpy as jnp
from jax import lax
from jax.experimental import pallas as pl
from jax.experimental.pallas import tpu as pltpu
from jax.sharding import PartitionSpec as P

BF16 = jnp.bfloat16
F32 = jnp.float32


def dot(left, right):
    return jnp.dot(left, right, preferred_element_type=F32)


def dot_t(left, right):
    return lax.dot_general(left, right, (((1,), (1,)), ((), ())), preferred_element_type=F32)


def split(values):
    high = values.astype(BF16)
    return high, (values - high.astype(F32)).astype(BF16)


def wide_dot(values, weight, product):
    rows = values.shape[0]
    high, low = split(values)
    both = product(jnp.concatenate([high.astype(F32), low.astype(F32)], axis=0).astype(BF16), weight)
    return both[:rows] + both[rows:]


def thirds(values):
    high, rest = values.astype(BF16), values
    rest = rest - high.astype(F32)
    mid = rest.astype(BF16).astype(F32)
    low = (rest - mid).astype(BF16).astype(F32)
    return jnp.concatenate([high.astype(F32), mid, low], axis=0).astype(BF16)


def layer_norm(values, gain):
    average = jnp.mean(values, axis=-1, keepdims=True)
    centred = values - average
    spread = jnp.mean(centred * centred, axis=-1, keepdims=True)
    inv_std = lax.rsqrt(spread + 1e-05)
    normed = centred * inv_std
    return normed * gain, normed, inv_std


def norm_back(normed, inv_std, gain, upstream):
    scaled = upstream * gain
    return inv_std * (
        scaled
        - jnp.mean(scaled, axis=-1, keepdims=True)
        - normed * jnp.mean(scaled * normed, axis=-1, keepdims=True)
    )


def call(body, out, *args, flops=1e8, limit=16):
    return pl.pallas_call(
        body,
        out_shape=out,
        in_specs=[pl.BlockSpec(memory_space=pltpu.VMEM)] * len(args),
        out_specs=jax.tree.map(lambda _: pl.BlockSpec(memory_space=pltpu.VMEM), out),
        compiler_params=pltpu.CompilerParams(vmem_limit_bytes=limit * 2**20),
        cost_estimate=pl.CostEstimate(flops=int(flops), bytes_accessed=2**20, transcendentals=0),
    )(*args)


def silu_parts(values):
    sigma = 0.5 + 0.5 * jnp.tanh(0.5 * values)
    hidden = values * sigma
    return hidden.astype(BF16), sigma * (1.0 + (values - hidden))


def prep_kernel(mesh_ref, grid_ref, src_ref, peer_ref, slot_ref, tiled_ref, pack_ref):
    count, latent = mesh_ref.shape
    times = tiled_ref.shape[0] // count
    rows = mesh_ref[...].astype(F32)
    tiled_ref[...] = jnp.concatenate([rows] * times, axis=0).astype(BF16)
    grids = grid_ref.shape[0]
    pack_ref[:grids, :] = grid_ref[...]
    spare = pack_ref.shape[0] - grids
    place = lax.broadcasted_iota(jnp.int32, (spare, latent), 0)
    index = jnp.where(place == 0, src_ref[...], jnp.where(place == 1, peer_ref[...], slot_ref[...]))
    pack_ref[grids:, :] = index.astype(F32).astype(BF16)


def src_kernel(own_ref, mate_ref, pick_ref, weight_ref, bias_ref, pre_ref):
    tile = own_ref.shape[0]
    edges = pick_ref.shape[0]
    for start in range(0, edges, tile):
        grid_ref = own_ref if start < edges // 2 else mate_ref
        rows = dot(pick_ref[start : start + tile, :], grid_ref[:tile, :]).astype(BF16)
        pre_ref[start : start + tile, :] = dot(rows, weight_ref[...]) + bias_ref[...]


def stack_split(values):
    high = values.astype(BF16).astype(F32)
    return jnp.concatenate([high, values - high], axis=0).astype(BF16)


def enc_kernel(pre_ref, dst_ref, dst_t_ref, mesh_ref, weight_ref, sum_ref, slope_ref):
    tile = 256
    latent = pre_ref.shape[1]
    plane_nodes = mesh_ref.shape[0]
    table = stack_split(dot(mesh_ref[...], weight_ref[...]))
    total = None
    for start in range(0, pre_ref.shape[0], tile):
        pre = pre_ref[start : start + tile, :] + dot(dst_ref[start : start + tile, :], table)
        hidden, slope = silu_parts(pre)
        slope_ref[start : start + tile, :] = slope
        both = jnp.concatenate([hidden, slope.astype(BF16)], axis=1)
        part = dot(dst_t_ref[:, start : start + tile], both)
        total = part if total is None else total + part
    nodes = sum_ref.shape[1] // 2
    chunked = lambda v: v.reshape(plane_nodes // nodes, nodes, latent)
    sum_ref[...] = jnp.concatenate(
        [chunked(total[:, :latent]), chunked(total[:, latent:])], axis=1
    ).astype(BF16)


def mid_kernel(parts_ref, weight_ref, gain_ref, mesh_ref, mid_ref, agg_ref, slopes_ref):
    count = mesh_ref.shape[0]
    summed = jnp.sum(parts_ref[...].astype(F32), axis=0)
    agg = wide_dot(summed[:count], weight_ref[...], dot)
    slopes_ref[...] = summed[count:]
    agg_ref[...] = agg
    mid_ref[...] = (mesh_ref[...].astype(F32) + layer_norm(agg, gain_ref[...])[0]).astype(BF16)


def proc_kernel(
    one_ref, mid_ref, two_ref, pick_ref, pick_t_ref, src_w_ref, dst_w_ref, out_w_ref, bias_ref,
    gain_ref, cotangent_ref, out_ref, rim_one_ref, rim_two_ref, grad_ref,
):
    count = mid_ref.shape[0]
    mid = mid_ref[...].astype(F32)
    near = jnp.concatenate([one_ref[...].astype(F32), mid, two_ref[...].astype(F32)], axis=0)
    table = jnp.concatenate(
        [dot(near.astype(BF16), src_w_ref[...]), dot(mid.astype(BF16), dst_w_ref[...]) + bias_ref[...]],
        axis=0,
    )
    hidden, slope = silu_parts(dot(pick_ref[...], thirds(table)))
    summed = dot(pick_t_ref[...], hidden)[3 * count :]
    agg = wide_dot(summed, out_w_ref[...], dot)
    shifted, normed, inv_std = layer_norm(agg, gain_ref[...])
    out_ref[...] = (mid + shifted).astype(BF16)
    upstream = cotangent_ref[...].astype(F32)
    grad_agg = norm_back(normed, inv_std, gain_ref[...], upstream).astype(BF16)
    back = dot_t(grad_agg, out_w_ref[...])
    blank = jnp.zeros((3 * count, back.shape[1]), F32)
    spread = dot(pick_ref[...], thirds(jnp.concatenate([blank, back], axis=0)))
    pre_grad = (spread * slope).astype(BF16)
    sums = dot(pick_t_ref[...], pre_grad)
    sender = wide_dot(sums[: 3 * count], src_w_ref[...], dot_t)
    receiver = wide_dot(sums[3 * count :], dst_w_ref[...], dot_t)
    rim_one_ref[...] = sender[:count].astype(BF16)
    rim_two_ref[...] = sender[2 * count :].astype(BF16)
    grad_ref[...] = upstream + receiver + sender[count : 2 * count]


def back_kernel(part_ref, one_ref, two_ref, agg_ref, gain_ref, grad_ref, tiled_ref):
    grad = part_ref[...] + one_ref[...].astype(F32) + two_ref[...].astype(F32)
    grad_ref[...] = grad
    _, normed, inv_std = layer_norm(agg_ref[...], gain_ref[...])
    rows = norm_back(normed, inv_std, gain_ref[...], grad)
    times = tiled_ref.shape[0] // rows.shape[0]
    tiled_ref[...] = jnp.concatenate([rows] * times, axis=0).astype(BF16)


def mesh_kernel(tiled_ref, slopes_ref, grad_ref, out_w_ref, dst_w_ref, out_ref):
    count = grad_ref.shape[0]
    rows = dot_t(tiled_ref[: 2 * count, :], out_w_ref[...])[:count]
    out_ref[...] = (
        grad_ref[...] + wide_dot(rows * slopes_ref[...], dst_w_ref[...], dot_t)
    ).astype(BF16)


def mate_kernel(grad_ref, dst_ref, pick_t_ref, slope_ref, out_w_ref, src_w_ref, table_ref, part_ref):
    half = dst_ref.shape[0] // 2
    table = stack_split(dot_t(grad_ref[...], out_w_ref[...]))
    table_ref[...] = table
    edge = (dot(dst_ref[half:, :], table) * slope_ref[half:, :]).astype(BF16)
    summed = dot(pick_t_ref[:, half:], edge)
    part_ref[...] = wide_dot(summed, src_w_ref[...], dot_t).astype(BF16)


def own_kernel(table_ref, dst_ref, pick_t_ref, slope_ref, src_w_ref, part_ref):
    half = dst_ref.shape[0] // 2
    edge = (dot(dst_ref[:half, :], table_ref[...]) * slope_ref[:half, :]).astype(BF16)
    summed = dot(pick_t_ref[:, :half], edge)
    part_ref[...] = wide_dot(summed, src_w_ref[...], dot_t)


def join_kernel(own_ref, mate_ref, out_ref):
    out_ref[...] = (own_ref[...] + mate_ref[...].astype(F32)).astype(BF16)


def per_device(
    grid_latent,
    mesh_latent,
    g2m_src,
    g2m_peer,
    g2m_slot,
    proc_src,
    proc_dst,
    enc_src_w,
    enc_dst_w,
    enc_out_w,
    enc_bias,
    enc_gain,
    proc_src_w,
    proc_dst_w,
    proc_out_w,
    proc_bias,
    proc_gain,
    cotangent,
):
    feats = lax.axis_size("feat")
    bands = lax.axis_size("band")
    chips = feats // 2
    core = lax.axis_index("feat") % 2
    band = lax.axis_index("band")
    edges = g2m_src.shape[0]
    grids, latent = grid_latent.shape
    nodes = mesh_latent.shape[0]
    plane_nodes = chips * nodes
    plane = [[2 * chip + side for chip in range(chips)] for side in range(2)]
    shape = jax.ShapeDtypeStruct
    row = lambda vector: vector.reshape(1, latent)

    def exchange(values):
        return lax.all_to_all(
            values.reshape(chips, -1, latent), "feat", split_axis=0, concat_axis=0, tiled=True,
            axis_index_groups=plane,
        )

    def swap(values):
        return lax.ppermute(values, "feat", [(i, i ^ 1) for i in range(feats)])

    first = [(i, i ^ 1) for i in range(bands)]
    second = [(i, j) for i in range(1, bands - 2, 2) for i, j in ((i, i + 1), (i + 1, i))]
    line = lambda index: index.reshape(1, edges)

    tiled_mesh, pack = call(
        prep_kernel, (shape((plane_nodes, latent), BF16), shape((grids + 16, latent), BF16)),
        mesh_latent, grid_latent, line(g2m_src), line(g2m_peer), line(g2m_slot),
    )
    mate_pack = swap(pack)
    mesh_all = exchange(tiled_mesh).reshape(plane_nodes, latent)

    mate_index = mate_pack[grids : grids + 3].astype(jnp.int32)
    joined = lambda own, place: jnp.concatenate([own, mate_index[place]])
    source, peer, slot = joined(g2m_src, 0), joined(g2m_peer[:, 0], 1), joined(g2m_slot, 2)
    target = jnp.where(peer % 2 == core, peer // 2 * nodes + slot, -1)
    grid_ids = jnp.arange(grids, dtype=jnp.int32)
    node_ids = jnp.arange(plane_nodes, dtype=jnp.int32)
    src_pick = (source[:, None] == grid_ids[None, :]).astype(BF16)
    src_pick_t = (source[None, :] == grid_ids[:, None]).astype(BF16)
    dst_pick = (target[:, None] == jnp.tile(node_ids, 2)[None, :]).astype(BF16)
    dst_pick_t = (target[None, :] == node_ids[:, None]).astype(BF16)

    side = proc_src // nodes
    sender = jnp.where(band % 2 == 0, 2 - side, side) * nodes + proc_src % nodes
    table_ids = jnp.arange(4 * nodes, dtype=jnp.int32)

    def proc_pick(ids, per_edge):
        return jnp.logical_or(per_edge(sender) == ids, per_edge(proc_dst + 3 * nodes) == ids).astype(BF16)

    pick = proc_pick(jnp.tile(table_ids, 3)[None, :], lambda v: v[:, None])
    pick_t = proc_pick(table_ids[:, None], lambda v: v[None, :])

    pre_src = call(
        src_kernel, shape((2 * edges, latent), F32),
        grid_latent, mate_pack, src_pick, enc_src_w, row(enc_bias), flops=8e8,
    )
    partial, slope = call(
        enc_kernel,
        (shape((chips, 2 * nodes, latent), BF16), shape((2 * edges, latent), F32)),
        pre_src, dst_pick, dst_pick_t, mesh_all, enc_dst_w, flops=1.2e9,
    )
    mid, enc_agg, slopes = call(
        mid_kernel,
        (shape((nodes, latent), BF16), shape((nodes, latent), F32), shape((nodes, latent), F32)),
        exchange(partial), enc_out_w, row(enc_gain), mesh_latent,
    )
    one = lax.ppermute(mid, "band", first)
    two = lax.ppermute(mid, "band", second)
    mesh_out, rim_one, rim_two, grad_part = call(
        proc_kernel,
        (shape((nodes, latent), BF16),) * 3 + (shape((nodes, latent), F32),),
        one, mid, two, pick, pick_t, proc_src_w, proc_dst_w, proc_out_w, row(proc_bias),
        row(proc_gain), cotangent,
    )
    back_one = lax.ppermute(rim_one, "band", first)
    back_two = lax.ppermute(rim_two, "band", second)
    grad_mid, tiled = call(
        back_kernel, (shape((nodes, latent), F32), shape((plane_nodes, latent), BF16)),
        grad_part, back_one, back_two, enc_agg, row(enc_gain),
    )
    grad_all = exchange(tiled).reshape(plane_nodes, latent)
    grad_mesh = call(
        mesh_kernel, shape((nodes, latent), BF16), tiled, slopes, grad_mid, enc_out_w, enc_dst_w,
    )
    table, mate_grad = call(
        mate_kernel, (shape((2 * plane_nodes, latent), BF16), shape((grids, latent), BF16)),
        grad_all, dst_pick, src_pick_t, slope, enc_out_w, enc_src_w, flops=8e8,
    )
    own_grad = call(
        own_kernel, shape((grids, latent), F32),
        table, dst_pick, src_pick_t, slope, enc_src_w, flops=6e8,
    )
    grad_grid = call(join_kernel, shape((grids, latent), BF16), own_grad, swap(mate_grad))
    return (mesh_out, grad_grid, grad_mesh)


def solution(mesh):
    shard = ("band", "feat")
    placed = (P(shard, None), P(shard, None), P(shard), P(shard, None), P(shard), P(shard), P(shard))
    placed += (P(),) * 10 + (P(shard, None),)
    return jax.shard_map(
        per_device,
        mesh=mesh,
        in_specs=placed,
        out_specs=(P(shard, None), P(shard, None), P(shard, None)),
        check_vma=False,
    )
```

```python
import jax
import jax.numpy as jnp
from jax import lax
from jax.experimental import pallas as pl
from jax.experimental.pallas import tpu as pltpu
from jax.sharding import PartitionSpec as P

BF16 = jnp.bfloat16
F32 = jnp.float32


def dot(left, right):
    return jnp.dot(left, right, preferred_element_type=F32)


def dot_t(left, right):
    return lax.dot_general(left, right, (((1,), (1,)), ((), ())), preferred_element_type=F32)


def split(values):
    high = values.astype(BF16)
    return high, (values - high.astype(F32)).astype(BF16)


def wide_dot(values, weight, product):
    rows = values.shape[0]
    high, low = split(values)
    both = product(jnp.concatenate([high.astype(F32), low.astype(F32)], axis=0).astype(BF16), weight)
    return both[:rows] + both[rows:]


def thirds(values):
    high, rest = values.astype(BF16), values
    rest = rest - high.astype(F32)
    mid = rest.astype(BF16).astype(F32)
    low = (rest - mid).astype(BF16).astype(F32)
    return jnp.concatenate([high.astype(F32), mid, low], axis=0).astype(BF16)


def layer_norm(values, gain):
    average = jnp.mean(values, axis=-1, keepdims=True)
    centred = values - average
    spread = jnp.mean(centred * centred, axis=-1, keepdims=True)
    inv_std = lax.rsqrt(spread + 1e-05)
    normed = centred * inv_std
    return normed * gain, normed, inv_std


def norm_back(normed, inv_std, gain, upstream):
    scaled = upstream * gain
    return inv_std * (
        scaled
        - jnp.mean(scaled, axis=-1, keepdims=True)
        - normed * jnp.mean(scaled * normed, axis=-1, keepdims=True)
    )


def call(body, out, *args, far=(), far_out=(), scratch=(), limit=16, cost=1):
    place = lambda there: pl.BlockSpec(memory_space=pltpu.HBM if there else pltpu.VMEM)
    single = not isinstance(out, tuple)
    outs = (out,) if single else out
    out_specs = tuple(place(i in far_out) for i in range(len(outs)))
    outs = tuple(
        pltpu.HBM(one.shape, one.dtype) if i in far_out else one for i, one in enumerate(outs)
    )
    args = tuple(
        pltpu.with_memory_space_constraint(arg, pltpu.HBM) if i in far else arg
        for i, arg in enumerate(args)
    )
    return pl.pallas_call(
        body,
        out_shape=outs[0] if single else outs,
        in_specs=[place(i in far) for i in range(len(args))],
        out_specs=out_specs[0] if single else out_specs,
        scratch_shapes=scratch,
        compiler_params=pltpu.CompilerParams(vmem_limit_bytes=limit * 2**20 or None),
        cost_estimate=pl.CostEstimate(
            flops=cost * 4 * 10**9, bytes_accessed=cost * 2**22, transcendentals=0
        ),
    )(*args)


def row_copies(source, target, sems, tile, offset=0):
    return [
        pltpu.make_async_copy(
            source.at[offset + i * tile : offset + (i + 1) * tile, :],
            target.at[i * tile : (i + 1) * tile, :],
            sems.at[i],
        )
        for i in range(sems.shape[0])
    ]


def silu_parts(values):
    sigma = 0.5 + 0.5 * jnp.tanh(0.5 * values)
    hidden = values * sigma
    return hidden.astype(BF16), sigma * (1.0 + (values - hidden))


def prep_kernel(
    mesh_ref, grid_ref, src_ref, peer_ref, slot_ref, tiled_ref, pack_ref, mesh_buf, index_buf, sems
):
    count, latent = mesh_buf.shape
    grids = grid_ref.shape[0]
    copies = [
        pltpu.make_async_copy(mesh_ref, mesh_buf, sems.at[0]),
        pltpu.make_async_copy(src_ref, index_buf.at[0], sems.at[1]),
        pltpu.make_async_copy(peer_ref, index_buf.at[1], sems.at[2]),
        pltpu.make_async_copy(slot_ref, index_buf.at[2], sems.at[3]),
        pltpu.make_async_copy(grid_ref, pack_ref.at[:grids, :], sems.at[4]),
    ]
    for copy in copies:
        copy.start()
    for copy in copies[:4]:
        copy.wait()
    times = tiled_ref.shape[0] // count
    rows = mesh_buf[...].astype(F32)
    tiled_ref[...] = jnp.concatenate([rows] * times, axis=0).astype(BF16)
    spare = pack_ref.shape[0] - grids
    place = lax.broadcasted_iota(jnp.int32, (spare, latent), 0)
    index = jnp.where(place == 0, index_buf[0], jnp.where(place == 1, index_buf[1], index_buf[2]))
    pack_ref[grids:, :] = index.astype(F32).astype(BF16)
    copies[4].wait()


def src_kernel(own_ref, mate_ref, pick_ref, weight_ref, bias_ref, pre_ref, buf, sems):
    tile = own_ref.shape[0]
    copies = row_copies(buf, pre_ref, sems, tile)
    for i, copy in enumerate(copies):
        grid_ref = own_ref if i < len(copies) // 2 else mate_ref
        rows = dot(pick_ref[i * tile : (i + 1) * tile, :], grid_ref[:tile, :]).astype(BF16)
        buf[i * tile : (i + 1) * tile, :] = dot(rows, weight_ref[...]) + bias_ref[...]
        copy.start()
    for copy in copies:
        copy.wait()


def stack_split(values):
    high = values.astype(BF16).astype(F32)
    return jnp.concatenate([high, values - high], axis=0).astype(BF16)


def spread_rows(pick, table):
    half = table.shape[0] // 2
    return dot(pick, table[:half]) + dot(pick, table[half:])


def enc_kernel(
    pre_ref, dst_ref, dst_t_ref, mesh_ref, weight_ref, sum_ref, slope_ref,
    pre_buf, slope_buf, both, in_sems, out_sems,
):
    latent = weight_ref.shape[1]
    plane_nodes = mesh_ref.shape[0]
    tile = pre_buf.shape[0] // in_sems.shape[0]
    arriving = row_copies(pre_ref, pre_buf, in_sems, tile)
    leaving = row_copies(slope_buf, slope_ref, out_sems, tile)
    for copy in arriving:
        copy.start()
    table = stack_split(dot(mesh_ref[...], weight_ref[...]))
    for i in range(len(arriving)):
        rows = slice(i * tile, (i + 1) * tile)
        spread = spread_rows(dst_ref[rows, :], table)
        arriving[i].wait()
        hidden, slope = silu_parts(pre_buf[rows, :] + spread)
        slope_buf[rows, :] = slope
        leaving[i].start()
        both[rows, :latent] = hidden
        both[rows, latent:] = slope.astype(BF16)
    total = dot(dst_t_ref[...], both[...])
    nodes = sum_ref.shape[1] // 2
    chunked = lambda v: v.reshape(plane_nodes // nodes, nodes, latent)
    sum_ref[...] = jnp.concatenate(
        [chunked(total[:, :latent]), chunked(total[:, latent:])], axis=1
    ).astype(BF16)
    for copy in leaving:
        copy.wait()


def mid_kernel(parts_ref, weight_ref, gain_ref, mesh_ref, mid_ref, agg_ref, slopes_ref):
    count = mesh_ref.shape[0]
    summed = jnp.sum(parts_ref[...].astype(F32), axis=0)
    agg = wide_dot(summed[:count], weight_ref[...], dot)
    slopes_ref[...] = summed[count:]
    agg_ref[...] = agg
    mid_ref[...] = (mesh_ref[...].astype(F32) + layer_norm(agg, gain_ref[...])[0]).astype(BF16)


def proc_kernel(
    one_ref, mid_ref, two_ref, pick_ref, pick_t_ref, src_w_ref, dst_w_ref, out_w_ref, bias_ref,
    gain_ref, cotangent_ref, out_ref, rim_one_ref, rim_two_ref, grad_ref,
):
    count = mid_ref.shape[0]
    mid = mid_ref[...].astype(F32)
    near = jnp.concatenate([one_ref[...].astype(F32), mid, two_ref[...].astype(F32)], axis=0)
    table = jnp.concatenate(
        [dot(near.astype(BF16), src_w_ref[...]), dot(mid.astype(BF16), dst_w_ref[...]) + bias_ref[...]],
        axis=0,
    )
    hidden, slope = silu_parts(dot(pick_ref[...], thirds(table)))
    summed = dot(pick_t_ref[...], hidden)[3 * count :]
    agg = wide_dot(summed, out_w_ref[...], dot)
    shifted, normed, inv_std = layer_norm(agg, gain_ref[...])
    out_ref[...] = (mid + shifted).astype(BF16)
    upstream = cotangent_ref[...].astype(F32)
    grad_agg = norm_back(normed, inv_std, gain_ref[...], upstream).astype(BF16)
    back = dot_t(grad_agg, out_w_ref[...])
    blank = jnp.zeros((3 * count, back.shape[1]), F32)
    spread = dot(pick_ref[...], thirds(jnp.concatenate([blank, back], axis=0)))
    pre_grad = (spread * slope).astype(BF16)
    sums = dot(pick_t_ref[...], pre_grad)
    sender = wide_dot(sums[: 3 * count], src_w_ref[...], dot_t)
    receiver = wide_dot(sums[3 * count :], dst_w_ref[...], dot_t)
    rim_one_ref[...] = sender[:count].astype(BF16)
    rim_two_ref[...] = sender[2 * count :].astype(BF16)
    grad_ref[...] = upstream + receiver + sender[count : 2 * count]


def back_kernel(part_ref, one_ref, two_ref, agg_ref, gain_ref, grad_ref, tiled_ref):
    grad = part_ref[...] + one_ref[...].astype(F32) + two_ref[...].astype(F32)
    grad_ref[...] = grad
    _, normed, inv_std = layer_norm(agg_ref[...], gain_ref[...])
    rows = norm_back(normed, inv_std, gain_ref[...], grad)
    times = tiled_ref.shape[0] // rows.shape[0]
    tiled_ref[...] = jnp.concatenate([rows] * times, axis=0).astype(BF16)


def mesh_kernel(tiled_ref, slopes_ref, grad_ref, out_w_ref, dst_w_ref, out_ref):
    count = grad_ref.shape[0]
    rows = dot_t(tiled_ref[: 2 * count, :], out_w_ref[...])[:count]
    out_ref[...] = (
        grad_ref[...] + wide_dot(rows * slopes_ref[...], dst_w_ref[...], dot_t)
    ).astype(BF16)


def mate_kernel(
    grad_ref, dst_ref, pick_t_ref, slope_ref, out_w_ref, src_w_ref, table_ref, part_ref, buf, sems
):
    half = dst_ref.shape[0] // 2
    tile = half // sems.shape[0]
    arriving = row_copies(slope_ref, buf, sems, tile, half)
    for copy in arriving:
        copy.start()
    table = stack_split(dot_t(grad_ref[...], out_w_ref[...]))
    table_ref[...] = table
    spread = spread_rows(dst_ref[half:, :], table)
    for copy in arriving:
        copy.wait()
    summed = dot(pick_t_ref[:, half:], (spread * buf[...]).astype(BF16))
    part_ref[...] = wide_dot(summed, src_w_ref[...], dot_t).astype(BF16)


def own_kernel(table_ref, dst_ref, pick_t_ref, slope_ref, src_w_ref, part_ref, buf, sems):
    half = dst_ref.shape[0] // 2
    tile = half // sems.shape[0]
    arriving = row_copies(slope_ref, buf, sems, tile)
    for copy in arriving:
        copy.start()
    spread = spread_rows(dst_ref[:half, :], table_ref[...])
    for copy in arriving:
        copy.wait()
    summed = dot(pick_t_ref[:, :half], (spread * buf[...]).astype(BF16))
    part_ref[...] = wide_dot(summed, src_w_ref[...], dot_t)


def join_kernel(own_ref, mate_ref, out_ref):
    out_ref[...] = (own_ref[...] + mate_ref[...].astype(F32)).astype(BF16)


def per_device(
    grid_latent,
    mesh_latent,
    g2m_src,
    g2m_peer,
    g2m_slot,
    proc_src,
    proc_dst,
    enc_src_w,
    enc_dst_w,
    enc_out_w,
    enc_bias,
    enc_gain,
    proc_src_w,
    proc_dst_w,
    proc_out_w,
    proc_bias,
    proc_gain,
    cotangent,
):
    feats = lax.axis_size("feat")
    bands = lax.axis_size("band")
    chips = feats // 2
    core = lax.axis_index("feat") % 2
    band = lax.axis_index("band")
    edges = g2m_src.shape[0]
    grids, latent = grid_latent.shape
    nodes = mesh_latent.shape[0]
    plane_nodes = chips * nodes
    plane = [[2 * chip + side for chip in range(chips)] for side in range(2)]
    shape = jax.ShapeDtypeStruct
    row = lambda vector: vector.reshape(1, latent)

    def exchange(values):
        return lax.all_to_all(
            values.reshape(chips, -1, latent), "feat", split_axis=0, concat_axis=0, tiled=True,
            axis_index_groups=plane,
        )

    def swap(values):
        return lax.ppermute(values, "feat", [(i, i ^ 1) for i in range(feats)])

    first = [(i, i ^ 1) for i in range(bands)]
    second = [(i, j) for i in range(1, bands - 2, 2) for i, j in ((i, i + 1), (i + 1, i))]
    line = lambda index: index.reshape(1, edges)
    sem = lambda count: pltpu.SemaphoreType.DMA((count,))
    wide = pltpu.VMEM((2 * edges, latent), F32)

    tiled_mesh, pack = call(
        prep_kernel, (shape((plane_nodes, latent), BF16), shape((grids + 16, latent), BF16)),
        mesh_latent, grid_latent, line(g2m_src), line(g2m_peer), line(g2m_slot),
        far=range(5),
        scratch=(pltpu.VMEM((nodes, latent), BF16), pltpu.VMEM((3, 1, edges), jnp.int32), sem(5)),
    )
    mate_pack = swap(pack)
    mesh_all = exchange(tiled_mesh).reshape(plane_nodes, latent)

    mate_index = mate_pack[grids : grids + 3].astype(jnp.int32)
    joined = lambda own, place: jnp.concatenate([own, mate_index[place]])
    source, peer, slot = joined(g2m_src, 0), joined(g2m_peer[:, 0], 1), joined(g2m_slot, 2)
    target = jnp.where(peer % 2 == core, peer // 2 * nodes + slot, -1)
    grid_ids = jnp.arange(grids, dtype=jnp.int32)
    node_ids = jnp.arange(plane_nodes, dtype=jnp.int32)
    src_pick = (source[:, None] == grid_ids[None, :]).astype(BF16)
    src_pick_t = (source[None, :] == grid_ids[:, None]).astype(BF16)
    dst_pick = (target[:, None] == node_ids[None, :]).astype(BF16)
    dst_pick_t = (target[None, :] == node_ids[:, None]).astype(BF16)

    side = proc_src // nodes
    sender = jnp.where(band % 2 == 0, 2 - side, side) * nodes + proc_src % nodes
    table_ids = jnp.arange(4 * nodes, dtype=jnp.int32)

    def proc_pick(ids, per_edge):
        return jnp.logical_or(per_edge(sender) == ids, per_edge(proc_dst + 3 * nodes) == ids).astype(BF16)

    pick = proc_pick(jnp.tile(table_ids, 3)[None, :], lambda v: v[:, None])
    pick_t = proc_pick(table_ids[:, None], lambda v: v[None, :])

    pre_src = call(
        src_kernel, shape((2 * edges, latent), F32),
        grid_latent, mate_pack, src_pick, enc_src_w, row(enc_bias),
        far_out=(0,), scratch=(wide, sem(4)),
    )
    partial, slope = call(
        enc_kernel,
        (shape((chips, 2 * nodes, latent), BF16), shape((2 * edges, latent), F32)),
        pre_src, dst_pick, dst_pick_t, mesh_all, enc_dst_w,
        far=(0,), far_out=(1,), limit=16,
        scratch=(wide, wide, pltpu.VMEM((2 * edges, 2 * latent), BF16), sem(4), sem(4)),
    )
    mid, enc_agg, slopes = call(
        mid_kernel,
        (shape((nodes, latent), BF16), shape((nodes, latent), F32), shape((nodes, latent), F32)),
        exchange(partial), enc_out_w, row(enc_gain), mesh_latent,
    )
    one = lax.ppermute(mid, "band", first)
    two = lax.ppermute(mid, "band", second)
    mesh_out, rim_one, rim_two, grad_part = call(
        proc_kernel,
        (shape((nodes, latent), BF16),) * 3 + (shape((nodes, latent), F32),),
        one, mid, two, pick, pick_t, proc_src_w, proc_dst_w, proc_out_w, row(proc_bias),
        row(proc_gain), cotangent,
    )
    back_one = lax.ppermute(rim_one, "band", first)
    back_two = lax.ppermute(rim_two, "band", second)
    grad_mid, tiled = call(
        back_kernel, (shape((nodes, latent), F32), shape((plane_nodes, latent), BF16)),
        grad_part, back_one, back_two, enc_agg, row(enc_gain),
    )
    grad_all = exchange(tiled).reshape(plane_nodes, latent)
    grad_mesh = call(
        mesh_kernel, shape((nodes, latent), BF16), tiled, slopes, grad_mid, enc_out_w, enc_dst_w,
    )
    table, mate_grad = call(
        mate_kernel, (shape((2 * plane_nodes, latent), BF16), shape((grids, latent), BF16)),
        grad_all, dst_pick, src_pick_t, slope, enc_out_w, enc_src_w, far=(3,), limit=16,
        scratch=(pltpu.VMEM((edges, latent), F32), sem(2)),
    )
    own_grad = call(
        own_kernel, shape((grids, latent), F32),
        table, dst_pick, src_pick_t, slope, enc_src_w, far=(3,), limit=16,
        scratch=(pltpu.VMEM((edges, latent), F32), sem(2)),
    )
    grad_grid = call(join_kernel, shape((grids, latent), BF16), own_grad, swap(mate_grad))
    return (mesh_out, grad_grid, grad_mesh)


def solution(mesh):
    shard = ("band", "feat")
    placed = (P(shard, None), P(shard, None), P(shard), P(shard, None), P(shard), P(shard), P(shard))
    placed += (P(),) * 10 + (P(shard, None),)
    return jax.shard_map(
        per_device,
        mesh=mesh,
        in_specs=placed,
        out_specs=(P(shard, None), P(shard, None), P(shard, None)),
        check_vma=False,
    )
```

```python
import jax
import jax.numpy as jnp
from jax import lax
from jax.experimental import pallas as pl
from jax.experimental.pallas import tpu as pltpu
from jax.sharding import PartitionSpec as P

BF16 = jnp.bfloat16
F32 = jnp.float32


def dot(left, right):
    return jnp.dot(left, right, preferred_element_type=F32)


def dot_t(left, right):
    return lax.dot_general(left, right, (((1,), (1,)), ((), ())), preferred_element_type=F32)


def split(values):
    high = values.astype(BF16)
    return high, (values - high.astype(F32)).astype(BF16)


def wide_dot(values, weight, product):
    rows = values.shape[0]
    high, low = split(values)
    both = product(jnp.concatenate([high.astype(F32), low.astype(F32)], axis=0).astype(BF16), weight)
    return both[:rows] + both[rows:]


def thirds(values):
    high, rest = values.astype(BF16), values
    rest = rest - high.astype(F32)
    mid = rest.astype(BF16).astype(F32)
    low = (rest - mid).astype(BF16).astype(F32)
    return jnp.concatenate([high.astype(F32), mid, low], axis=0).astype(BF16)


def layer_norm(values, gain):
    average = jnp.mean(values, axis=-1, keepdims=True)
    centred = values - average
    spread = jnp.mean(centred * centred, axis=-1, keepdims=True)
    inv_std = lax.rsqrt(spread + 1e-05)
    normed = centred * inv_std
    return normed * gain, normed, inv_std


def norm_back(normed, inv_std, gain, upstream):
    scaled = upstream * gain
    return inv_std * (
        scaled
        - jnp.mean(scaled, axis=-1, keepdims=True)
        - normed * jnp.mean(scaled * normed, axis=-1, keepdims=True)
    )


def call(body, out, *args, far=(), far_out=(), small=(), scratch=(), limit=16, cost=1):
    place = lambda there: pl.BlockSpec(memory_space=pltpu.HBM if there else pltpu.VMEM)
    single = not isinstance(out, tuple)
    outs = (out,) if single else out
    out_specs = tuple(place(i in far_out) for i in range(len(outs)))
    outs = tuple(
        pltpu.HBM(one.shape, one.dtype) if i in far_out else one for i, one in enumerate(outs)
    )
    args = tuple(
        pltpu.with_memory_space_constraint(arg, pltpu.HBM) if i in far else arg
        for i, arg in enumerate(args)
    )
    return pl.pallas_call(
        body,
        out_shape=outs[0] if single else outs,
        in_specs=[
            pl.BlockSpec(memory_space=pltpu.SMEM) if i in small else place(i in far)
            for i in range(len(args))
        ],
        out_specs=out_specs[0] if single else out_specs,
        scratch_shapes=scratch,
        compiler_params=pltpu.CompilerParams(vmem_limit_bytes=limit * 2**20 or None),
        cost_estimate=pl.CostEstimate(
            flops=cost * 4 * 10**9, bytes_accessed=cost * 2**22, transcendentals=0
        ),
    )(*args)


def dot_first(left, right):
    return lax.dot_general(left, right, (((0,), (0,)), ((), ())), preferred_element_type=F32)


def row_copies(source, target, sems, tile, offset=0):
    return [
        pltpu.make_async_copy(
            source.at[offset + i * tile : offset + (i + 1) * tile, :],
            target.at[i * tile : (i + 1) * tile, :],
            sems.at[i],
        )
        for i in range(sems.shape[0])
    ]


def silu_parts(values):
    sigma = 0.5 + 0.5 * jnp.tanh(0.5 * values)
    hidden = values * sigma
    return hidden.astype(BF16), sigma * (1.0 + (values - hidden))


def prep_kernel(
    mesh_ref, grid_ref, cotangent_ref, src_ref, peer_ref, slot_ref, sender_ref, receiver_ref,
    tiled_ref, pack_ref, near_ref, mesh_buf, cotangent_buf, index_buf, near_buf, sems,
):
    count, latent = mesh_buf.shape
    grids = grid_ref.shape[0]
    half = sender_ref.shape[1]
    pairs = (
        (mesh_ref, mesh_buf),
        (src_ref, index_buf.at[0]),
        (peer_ref, index_buf.at[1]),
        (slot_ref, index_buf.at[2]),
        (sender_ref, near_buf.at[:, :half]),
        (receiver_ref, near_buf.at[:, half:]),
        (cotangent_ref, cotangent_buf),
        (grid_ref, pack_ref.at[:grids, :]),
    )
    copies = [pltpu.make_async_copy(*pair, sems.at[i]) for i, pair in enumerate(pairs)]
    for copy in copies:
        copy.start()
    for copy in copies[:7]:
        copy.wait()
    times = tiled_ref.shape[0] // count
    rows = mesh_buf[...].astype(F32)
    tiled_ref[...] = jnp.concatenate([rows] * times, axis=0).astype(BF16)
    spare = pack_ref.shape[0] - grids
    place = lax.broadcasted_iota(jnp.int32, (spare, latent), 0)
    index = jnp.where(place == 0, index_buf[0], jnp.where(place == 1, index_buf[1], index_buf[2]))
    pack_ref[grids:, :] = index.astype(F32).astype(BF16)
    ends = jnp.broadcast_to(near_buf[...], (count, 2 * half)).astype(F32)
    near_ref[...] = jnp.concatenate([cotangent_buf[...].astype(F32), ends], axis=0).astype(BF16)
    copies[7].wait()


def src_kernel(own_ref, mate_ref, pick_ref, weight_ref, bias_ref, pre_ref, buf, sems):
    tile = own_ref.shape[0]
    copies = row_copies(buf, pre_ref, sems, tile)
    for i, copy in enumerate(copies):
        grid_ref = own_ref if i < len(copies) // 2 else mate_ref
        rows = dot(pick_ref[i * tile : (i + 1) * tile, :], grid_ref[:tile, :]).astype(BF16)
        buf[i * tile : (i + 1) * tile, :] = dot(rows, weight_ref[...]) + bias_ref[...]
        copy.start()
    for copy in copies:
        copy.wait()


def stack_split(values):
    high = values.astype(BF16).astype(F32)
    return jnp.concatenate([high, values - high], axis=0).astype(BF16)


def spread_rows(pick, table):
    half = table.shape[0] // 2
    return dot(pick, table[:half]) + dot(pick, table[half:])


def enc_kernel(
    pre_ref, dst_ref, mesh_ref, weight_ref, sum_ref, slope_ref,
    pre_buf, hidden_buf, slope_buf, in_sems, out_sems,
):
    latent = weight_ref.shape[1]
    plane_nodes = mesh_ref.shape[0]
    tile = pre_buf.shape[0] // in_sems.shape[0]
    arriving = row_copies(pre_ref, pre_buf, in_sems, tile)
    leaving = row_copies(slope_buf, slope_ref, out_sems, tile)
    for copy in arriving:
        copy.start()
    table = stack_split(dot(mesh_ref[...], weight_ref[...]))
    for i in range(len(arriving)):
        rows = slice(i * tile, (i + 1) * tile)
        spread = spread_rows(dst_ref[rows, :], table)
        arriving[i].wait()
        hidden, slope = silu_parts(pre_buf[rows, :] + spread)
        hidden_buf[rows, :] = hidden
        slope_buf[rows, :] = slope.astype(BF16)
        leaving[i].start()
    nodes = sum_ref.shape[1] // 2
    node_sums = lambda values: dot_first(dst_ref[...], values).reshape(-1, nodes, latent)
    sum_ref[...] = jnp.concatenate(
        [node_sums(hidden_buf[...]), node_sums(slope_buf[...])], axis=1
    ).astype(BF16)
    for copy in leaving:
        copy.wait()


def mid_kernel(
    parts_ref, weight_ref, gain_ref, mesh_ref, near_ref, mid_ref, packet_ref, agg_ref, slopes_ref
):
    count = mesh_ref.shape[0]
    summed = jnp.sum(parts_ref[...].astype(F32), axis=0)
    agg = wide_dot(summed[:count], weight_ref[...], dot)
    slopes_ref[...] = summed[count:]
    agg_ref[...] = agg
    mid = mesh_ref[...].astype(F32) + layer_norm(agg, gain_ref[...])[0]
    mid_ref[...] = mid.astype(BF16)
    packet_ref[...] = jnp.concatenate([mid, near_ref[...].astype(F32)], axis=0).astype(BF16)


def edge_ends(index, info_ref, offset, inside, group, count):
    half = index.shape[1] // 2
    source, receiver = index[:, :half], index[:, half:]
    bits = count.bit_length() - 1
    shift = offset + jnp.right_shift(source, bits) - 1
    one, two = info_ref[0], info_ref[1]
    spot = jnp.where(
        shift == 0, 4,
        jnp.where(
            shift == one, 0, jnp.where(shift == -one, 1, jnp.where(shift == two, 2, 3))
        ),
    )
    keep = lambda column: column * inside + (inside - 1)
    return (
        keep(spot * count + jnp.bitwise_and(source, count - 1)),
        keep((5 + group) * count + receiver),
    )


def proc_kernel(
    one_ref, two_ref, three_ref, four_ref, own_ref, info_ref, src_w_ref, dst_w_ref, out_w_ref,
    bias_ref, gain_ref, enc_agg_ref, enc_gain_ref, out_ref, grad_ref, tiled_ref,
):
    count = three_ref.shape[0]
    packets = [ref[...].astype(F32) for ref in (one_ref, two_ref, own_ref)]
    one, two, mid = (packet[:count] for packet in packets)
    upstreams = jnp.concatenate([packet[count : 2 * count] for packet in packets], axis=0)
    index = [packet[2 * count : 2 * count + 1].astype(jnp.int32) for packet in packets]
    step = info_ref[0]
    columns = [
        edge_ends(index[0], info_ref, step, info_ref[2], 0, count),
        edge_ends(index[1], info_ref, -step, info_ref[3], 1, count),
        edge_ends(index[2], info_ref, 0, 1, 2, count),
    ]
    sender, receiver = (jnp.concatenate(column, axis=1) for column in zip(*columns))
    ids = lax.broadcasted_iota(jnp.int32, (8 * count, sender.shape[1]), 0)
    chosen = jnp.where(jnp.logical_or(ids == sender, ids == receiver), 1.0, 0.0)
    pick_t = chosen.astype(BF16)
    pick = jnp.concatenate([chosen] * 3, axis=0).astype(BF16)

    rows = [one, two, three_ref[...].astype(F32), four_ref[...].astype(F32), mid]
    senders = jnp.concatenate(rows, axis=0).astype(BF16)
    receivers = jnp.concatenate([one, two, mid], axis=0).astype(BF16)
    table = jnp.concatenate(
        [dot(senders, src_w_ref[...]), dot(receivers, dst_w_ref[...]) + bias_ref[...]], axis=0
    )
    hidden, slope = silu_parts(dot_first(pick, thirds(table)))
    summed = dot(pick_t, hidden)[5 * count :]
    agg = wide_dot(summed, out_w_ref[...], dot)
    shifted, normed, inv_std = layer_norm(agg, gain_ref[...])
    out_ref[...] = (mid + shifted[2 * count :]).astype(BF16)
    grad_agg = norm_back(normed, inv_std, gain_ref[...], upstreams).astype(BF16)
    back = dot_t(grad_agg, out_w_ref[...])
    blank = jnp.zeros((5 * count, back.shape[1]), F32)
    spread = dot_first(pick, thirds(jnp.concatenate([blank, back], axis=0)))
    sums = dot(pick_t, (spread * slope).astype(BF16))
    sender_sum = wide_dot(sums[4 * count : 5 * count], src_w_ref[...], dot_t)
    receiver_sum = wide_dot(sums[7 * count :], dst_w_ref[...], dot_t)
    grad = upstreams[2 * count :] + receiver_sum + sender_sum
    grad_ref[...] = grad
    _, normed, inv_std = layer_norm(enc_agg_ref[...], enc_gain_ref[...])
    rows = norm_back(normed, inv_std, enc_gain_ref[...], grad)
    times = tiled_ref.shape[0] // count
    tiled_ref[...] = jnp.concatenate([rows] * times, axis=0).astype(BF16)


def mesh_kernel(tiled_ref, slopes_ref, grad_ref, out_w_ref, dst_w_ref, out_ref):
    count = grad_ref.shape[0]
    rows = dot_t(tiled_ref[: 2 * count, :], out_w_ref[...])[:count]
    out_ref[...] = (
        grad_ref[...] + wide_dot(rows * slopes_ref[...], dst_w_ref[...], dot_t)
    ).astype(BF16)


def mate_kernel(
    grad_ref, dst_ref, pick_t_ref, slope_ref, out_w_ref, src_w_ref, table_ref, part_ref, buf, sems
):
    half = dst_ref.shape[0] // 2
    (arriving,) = row_copies(slope_ref, buf, sems, half, half)
    arriving.start()
    table = stack_split(dot_t(grad_ref[...], out_w_ref[...]))
    table_ref[...] = table
    spread = spread_rows(dst_ref[half:, :], table)
    arriving.wait()
    edge = (spread * buf[...].astype(F32)).astype(BF16)
    part_ref[...] = wide_dot(dot(pick_t_ref[:, half:], edge), src_w_ref[...], dot_t).astype(BF16)


def own_kernel(table_ref, dst_ref, pick_t_ref, slope_ref, src_w_ref, part_ref, buf, sems):
    half = dst_ref.shape[0] // 2
    (arriving,) = row_copies(slope_ref, buf, sems, half)
    arriving.start()
    spread = spread_rows(dst_ref[:half, :], table_ref[...])
    arriving.wait()
    edge = (spread * buf[...].astype(F32)).astype(BF16)
    part_ref[...] = wide_dot(dot(pick_t_ref[:, :half], edge), src_w_ref[...], dot_t)


def join_kernel(own_ref, mate_ref, out_ref):
    out_ref[...] = (own_ref[...] + mate_ref[...].astype(F32)).astype(BF16)


def per_device(
    grid_latent,
    mesh_latent,
    g2m_src,
    g2m_peer,
    g2m_slot,
    proc_src,
    proc_dst,
    enc_src_w,
    enc_dst_w,
    enc_out_w,
    enc_bias,
    enc_gain,
    proc_src_w,
    proc_dst_w,
    proc_out_w,
    proc_bias,
    proc_gain,
    cotangent,
):
    feats = lax.axis_size("feat")
    bands = lax.axis_size("band")
    chips = feats // 2
    core = lax.axis_index("feat") % 2
    band = lax.axis_index("band")
    edges = g2m_src.shape[0]
    grids, latent = grid_latent.shape
    nodes = mesh_latent.shape[0]
    plane_nodes = chips * nodes
    plane = [[2 * chip + side for chip in range(chips)] for side in range(2)]
    shape = jax.ShapeDtypeStruct
    row = lambda vector: vector.reshape(1, latent)
    sem = lambda count: pltpu.SemaphoreType.DMA((count,))
    edge_buf = lambda count, kind: pltpu.VMEM((count, latent), kind)

    def exchange(values):
        return lax.all_to_all(
            values.reshape(chips, -1, latent), "feat", split_axis=0, concat_axis=0, tiled=True,
            axis_index_groups=plane,
        )

    def swap(values):
        return lax.ppermute(values, "feat", [(i, i ^ 1) for i in range(feats)])

    far_side = lambda step: [
        pair
        for i in range(bands - step)
        if i & step
        for pair in ((i, i + step), (i + step, i))
    ]
    near_side = lambda step: [(i, i ^ step) for i in range(bands)]
    line = lambda index: index.reshape(1, edges)

    tiled_mesh, pack, near = call(
        prep_kernel,
        (
            shape((plane_nodes, latent), BF16),
            shape((grids + 16, latent), BF16),
            shape((2 * nodes, latent), BF16),
        ),
        mesh_latent, grid_latent, cotangent, line(g2m_src), line(g2m_peer), line(g2m_slot),
        proc_src.reshape(1, -1), proc_dst.reshape(1, -1),
        far=range(8),
        scratch=(
            pltpu.VMEM((nodes, latent), BF16),
            pltpu.VMEM((nodes, latent), BF16),
            pltpu.VMEM((3, 1, edges), jnp.int32),
            pltpu.VMEM((1, latent), jnp.int32),
            pltpu.SemaphoreType.DMA((8,)),
        ),
    )
    mate_pack = swap(pack)
    mesh_all = exchange(tiled_mesh).reshape(plane_nodes, latent)

    mate_index = mate_pack[grids : grids + 3].astype(jnp.int32)
    joined = lambda own, place: jnp.concatenate([own, mate_index[place]])
    source, peer, slot = joined(g2m_src, 0), joined(g2m_peer[:, 0], 1), joined(g2m_slot, 2)
    target = jnp.where(peer % 2 == core, peer // 2 * nodes + slot, -1)
    grid_ids = jnp.arange(grids, dtype=jnp.int32)
    node_ids = jnp.arange(plane_nodes, dtype=jnp.int32)
    src_pick = (source[:, None] == grid_ids[None, :]).astype(BF16)
    src_pick_t = (source[None, :] == grid_ids[:, None]).astype(BF16)
    dst_pick = (target[:, None] == node_ids[None, :]).astype(BF16)

    step_one = jnp.where(band & 1 == 0, 1, -1)
    step_two = jnp.where(band & 2 == 0, 2, -2)
    inside = lambda place: jnp.logical_and(place >= 0, place < bands)
    info = jnp.stack([step_one, step_two, inside(band + step_one), inside(band - step_one)])

    pre_src = call(
        src_kernel, shape((2 * edges, latent), F32),
        grid_latent, mate_pack, src_pick, enc_src_w, row(enc_bias),
        far_out=(0,), scratch=(edge_buf(2 * edges, F32), sem(4)),
    )
    partial, slope = call(
        enc_kernel,
        (shape((chips, 2 * nodes, latent), BF16), shape((2 * edges, latent), BF16)),
        pre_src, dst_pick, mesh_all, enc_dst_w,
        far=(0,), far_out=(1,),
        scratch=(
            edge_buf(2 * edges, F32), edge_buf(2 * edges, BF16), edge_buf(2 * edges, BF16),
            sem(4), sem(4),
        ),
    )
    mid, packet, enc_agg, slopes = call(
        mid_kernel,
        (
            shape((nodes, latent), BF16),
            shape((3 * nodes, latent), BF16),
            shape((nodes, latent), F32),
            shape((nodes, latent), F32),
        ),
        exchange(partial), enc_out_w, row(enc_gain), mesh_latent, near,
    )
    mesh_out, grad_mid, tiled = call(
        proc_kernel,
        (
            shape((nodes, latent), BF16),
            shape((nodes, latent), F32),
            shape((plane_nodes, latent), BF16),
        ),
        lax.ppermute(packet, "band", near_side(1)),
        lax.ppermute(packet, "band", far_side(1)),
        lax.ppermute(mid, "band", near_side(2)),
        lax.ppermute(mid, "band", far_side(2)),
        packet, info.astype(jnp.int32), proc_src_w, proc_dst_w, proc_out_w, row(proc_bias),
        row(proc_gain), enc_agg, row(enc_gain),
        small=(5,),
    )
    grad_all = exchange(tiled).reshape(plane_nodes, latent)
    grad_mesh = call(
        mesh_kernel, shape((nodes, latent), BF16), tiled, slopes, grad_mid, enc_out_w, enc_dst_w,
    )
    table, mate_grad = call(
        mate_kernel, (shape((2 * plane_nodes, latent), BF16), shape((grids, latent), BF16)),
        grad_all, dst_pick, src_pick_t, slope, enc_out_w, enc_src_w,
        far=(3,), scratch=(edge_buf(edges, BF16), sem(1)),
    )
    own_grad = call(
        own_kernel, shape((grids, latent), F32), table, dst_pick, src_pick_t, slope, enc_src_w,
        far=(3,), scratch=(edge_buf(edges, BF16), sem(1)),
    )
    grad_grid = call(join_kernel, shape((grids, latent), BF16), own_grad, swap(mate_grad))
    return (mesh_out, grad_grid, grad_mesh)


def solution(mesh):
    shard = ("band", "feat")
    placed = (P(shard, None), P(shard, None), P(shard), P(shard, None), P(shard), P(shard), P(shard))
    placed += (P(),) * 10 + (P(shard, None),)
    return jax.shard_map(
        per_device,
        mesh=mesh,
        in_specs=placed,
        out_specs=(P(shard, None), P(shard, None), P(shard, None)),
        check_vma=False,
    )
```

```python
import jax
import jax.numpy as jnp
from jax import lax
from jax.experimental import pallas as pl
from jax.experimental.pallas import tpu as pltpu
from jax.sharding import PartitionSpec as P

BF16 = jnp.bfloat16
F32 = jnp.float32


def dot(left, right):
    return jnp.dot(left, right, preferred_element_type=F32)


def dot_t(left, right):
    return lax.dot_general(left, right, (((1,), (1,)), ((), ())), preferred_element_type=F32)


def split(values):
    high = values.astype(BF16)
    return high, (values - high.astype(F32)).astype(BF16)


def wide_dot(values, weight, product):
    rows = values.shape[0]
    high, low = split(values)
    both = product(jnp.concatenate([high.astype(F32), low.astype(F32)], axis=0).astype(BF16), weight)
    return both[:rows] + both[rows:]


def thirds(values):
    high, rest = values.astype(BF16), values
    rest = rest - high.astype(F32)
    mid = rest.astype(BF16).astype(F32)
    low = (rest - mid).astype(BF16).astype(F32)
    return jnp.concatenate([high.astype(F32), mid, low], axis=0).astype(BF16)


def layer_norm(values, gain):
    average = jnp.mean(values, axis=-1, keepdims=True)
    centred = values - average
    spread = jnp.mean(centred * centred, axis=-1, keepdims=True)
    inv_std = lax.rsqrt(spread + 1e-05)
    normed = centred * inv_std
    return normed * gain, normed, inv_std


def norm_back(normed, inv_std, gain, upstream):
    scaled = upstream * gain
    return inv_std * (
        scaled
        - jnp.mean(scaled, axis=-1, keepdims=True)
        - normed * jnp.mean(scaled * normed, axis=-1, keepdims=True)
    )


def call(body, out, *args, far=(), far_out=(), small=(), scratch=(), limit=16, cost=1):
    place = lambda there: pl.BlockSpec(memory_space=pltpu.HBM if there else pltpu.VMEM)
    single = not isinstance(out, tuple)
    outs = (out,) if single else out
    out_specs = tuple(place(i in far_out) for i in range(len(outs)))
    outs = tuple(
        pltpu.HBM(one.shape, one.dtype) if i in far_out else one for i, one in enumerate(outs)
    )
    args = tuple(
        pltpu.with_memory_space_constraint(arg, pltpu.HBM) if i in far else arg
        for i, arg in enumerate(args)
    )
    return pl.pallas_call(
        body,
        out_shape=outs[0] if single else outs,
        in_specs=[
            pl.BlockSpec(memory_space=pltpu.SMEM) if i in small else place(i in far)
            for i in range(len(args))
        ],
        out_specs=out_specs[0] if single else out_specs,
        scratch_shapes=scratch,
        compiler_params=pltpu.CompilerParams(vmem_limit_bytes=limit * 2**20 or None),
        cost_estimate=pl.CostEstimate(
            flops=cost * 4 * 10**9, bytes_accessed=cost * 2**22, transcendentals=0
        ),
    )(*args)


def dot_first(left, right):
    return lax.dot_general(left, right, (((0,), (0,)), ((), ())), preferred_element_type=F32)


def row_copies(source, target, sems, tile, offset=0):
    return [
        pltpu.make_async_copy(
            source.at[offset + i * tile : offset + (i + 1) * tile, :],
            target.at[i * tile : (i + 1) * tile, :],
            sems.at[i],
        )
        for i in range(sems.shape[0])
    ]


def silu_parts(values):
    sigma = 0.5 + 0.5 * jnp.tanh(0.5 * values)
    hidden = values * sigma
    return hidden.astype(BF16), sigma * (1.0 + (values - hidden))


def tile_kernel(mesh_ref, tiled_ref, sems):
    copies = [
        pltpu.make_async_copy(mesh_ref, tiled_ref.at[i], sems.at[i])
        for i in range(tiled_ref.shape[0])
    ]
    for copy in copies:
        copy.start()
    for copy in copies:
        copy.wait()


def prep_kernel(
    grid_ref, cotangent_ref, src_ref, peer_ref, slot_ref, sender_ref, receiver_ref,
    pack_ref, near_ref, cotangent_buf, index_buf, near_buf, pack_buf, sems,
):
    count, latent = cotangent_buf.shape
    grids = grid_ref.shape[0]
    half = sender_ref.shape[1]
    pairs = (
        (src_ref, index_buf.at[0]),
        (peer_ref, index_buf.at[1]),
        (slot_ref, index_buf.at[2]),
        (sender_ref, near_buf.at[:, :half]),
        (receiver_ref, near_buf.at[:, half:]),
        (cotangent_ref, cotangent_buf),
        (grid_ref, pack_ref.at[:grids, :]),
        (pack_buf, pack_ref.at[grids:, :]),
    )
    copies = [pltpu.make_async_copy(*pair, sems.at[i]) for i, pair in enumerate(pairs)]
    for copy in copies[:7]:
        copy.start()
    for copy in copies[:6]:
        copy.wait()
    place = lax.broadcasted_iota(jnp.int32, pack_buf.shape, 0)
    index = jnp.where(place == 0, index_buf[0], jnp.where(place == 1, index_buf[1], index_buf[2]))
    pack_buf[...] = index.astype(F32).astype(BF16)
    copies[7].start()
    ends = jnp.broadcast_to(near_buf[...], (count, 2 * half)).astype(F32)
    near_ref[...] = jnp.concatenate([cotangent_buf[...].astype(F32), ends], axis=0).astype(BF16)
    copies[6].wait()
    copies[7].wait()


def src_kernel(own_ref, mate_ref, pick_ref, weight_ref, bias_ref, pre_ref, buf, sems):
    tile = own_ref.shape[0]
    copies = row_copies(buf, pre_ref, sems, tile)
    for i, copy in enumerate(copies):
        grid_ref = own_ref if i < len(copies) // 2 else mate_ref
        rows = dot(pick_ref[i * tile : (i + 1) * tile, :], grid_ref[:tile, :]).astype(BF16)
        buf[i * tile : (i + 1) * tile, :] = dot(rows, weight_ref[...]) + bias_ref[...]
        copy.start()
    for copy in copies:
        copy.wait()


def stack_split(values):
    high = values.astype(BF16).astype(F32)
    return jnp.concatenate([high, values - high], axis=0).astype(BF16)


def spread_rows(pick, table):
    half = table.shape[0] // 2
    return dot(pick, table[:half]) + dot(pick, table[half:])


def enc_kernel(
    pre_ref, dst_ref, mesh_ref, weight_ref, sum_ref, slope_ref,
    pre_buf, hidden_buf, slope_buf, sum_buf, in_sems, slope_sem, sum_sems,
):
    latent = weight_ref.shape[1]
    tile = pre_buf.shape[0] // in_sems.shape[0]
    arriving = row_copies(pre_ref, pre_buf, in_sems, tile)
    (leaving,) = row_copies(slope_buf, slope_ref, slope_sem, slope_buf.shape[0])
    halves = [slice(0, latent), slice(latent, 2 * latent)]
    sums = [
        pltpu.make_async_copy(sum_buf.at[:, half], sum_ref.at[:, half], sum_sems.at[i])
        for i, half in enumerate(halves)
    ]
    arriving[0].start()
    arriving[1].start()
    table = stack_split(dot(mesh_ref[...], weight_ref[...]))
    for i in range(len(arriving)):
        rows = slice(i * tile, (i + 1) * tile)
        spread = spread_rows(dst_ref[rows, :], table)
        arriving[i].wait()
        if i + 2 < len(arriving):
            arriving[i + 2].start()
        hidden, slope = silu_parts(pre_buf[rows, :] + spread)
        hidden_buf[rows, :] = hidden
        slope_buf[rows, :] = slope.astype(BF16)
    for i, values in enumerate((hidden_buf, slope_buf)):
        sum_buf[:, halves[i]] = dot_first(dst_ref[...], values[...]).astype(BF16)
        sums[i].start()
    leaving.start()
    for copy in (*sums, leaving):
        copy.wait()


def mid_kernel(
    parts_ref, weight_ref, gain_ref, mesh_ref, near_ref, mid_ref, packet_ref, agg_ref, slopes_ref
):
    count = mesh_ref.shape[0]
    latent = mesh_ref.shape[1]
    summed = jnp.sum(parts_ref[...].astype(F32), axis=0)
    agg = wide_dot(summed[:, :latent], weight_ref[...], dot)
    slopes_ref[...] = summed[:, latent:]
    agg_ref[...] = agg
    mid = mesh_ref[...].astype(F32) + layer_norm(agg, gain_ref[...])[0]
    mid_ref[...] = mid.astype(BF16)
    packet_ref[...] = jnp.concatenate([mid, near_ref[...].astype(F32)], axis=0).astype(BF16)


def edge_ends(index, info_ref, offset, inside, group, count):
    half = index.shape[1] // 2
    source, receiver = index[:, :half], index[:, half:]
    bits = count.bit_length() - 1
    shift = offset + jnp.right_shift(source, bits) - 1
    one, two = info_ref[0], info_ref[1]
    spot = jnp.where(
        shift == 0, 4,
        jnp.where(
            shift == one, 0, jnp.where(shift == -one, 1, jnp.where(shift == two, 2, 3))
        ),
    )
    keep = lambda column: column * inside + (inside - 1)
    return (
        keep(spot * count + jnp.bitwise_and(source, count - 1)),
        keep((5 + group) * count + receiver),
    )


def proc_kernel(
    one_ref, two_ref, three_ref, four_ref, own_ref, info_ref, src_w_ref, dst_w_ref, out_w_ref,
    bias_ref, gain_ref, enc_agg_ref, enc_gain_ref, out_ref, grad_ref, tiled_ref,
):
    count = three_ref.shape[0]
    packets = [ref[...].astype(F32) for ref in (one_ref, two_ref, own_ref)]
    one, two, mid = (packet[:count] for packet in packets)
    upstreams = jnp.concatenate([packet[count : 2 * count] for packet in packets], axis=0)
    index = [packet[2 * count : 2 * count + 1].astype(jnp.int32) for packet in packets]
    step = info_ref[0]
    columns = [
        edge_ends(index[0], info_ref, step, info_ref[2], 0, count),
        edge_ends(index[1], info_ref, -step, info_ref[3], 1, count),
        edge_ends(index[2], info_ref, 0, 1, 2, count),
    ]
    sender, receiver = (jnp.concatenate(column, axis=1) for column in zip(*columns))
    ids = lax.broadcasted_iota(jnp.int32, (8 * count, sender.shape[1]), 0)
    chosen = jnp.where(jnp.logical_or(ids == sender, ids == receiver), 1.0, 0.0)
    pick_t = chosen.astype(BF16)
    pick = jnp.concatenate([chosen] * 3, axis=0).astype(BF16)

    rows = [one, two, three_ref[...].astype(F32), four_ref[...].astype(F32), mid]
    senders = jnp.concatenate(rows, axis=0).astype(BF16)
    receivers = jnp.concatenate([one, two, mid], axis=0).astype(BF16)
    table = jnp.concatenate(
        [dot(senders, src_w_ref[...]), dot(receivers, dst_w_ref[...]) + bias_ref[...]], axis=0
    )
    hidden, slope = silu_parts(dot_first(pick, thirds(table)))
    summed = dot(pick_t, hidden)[5 * count :]
    agg = wide_dot(summed, out_w_ref[...], dot)
    shifted, normed, inv_std = layer_norm(agg, gain_ref[...])
    out_ref[...] = (mid + shifted[2 * count :]).astype(BF16)
    grad_agg = norm_back(normed, inv_std, gain_ref[...], upstreams).astype(BF16)
    back = dot_t(grad_agg, out_w_ref[...])
    blank = jnp.zeros((5 * count, back.shape[1]), F32)
    spread = dot_first(pick, thirds(jnp.concatenate([blank, back], axis=0)))
    sums = dot(pick_t, (spread * slope).astype(BF16))
    sender_sum = wide_dot(sums[4 * count : 5 * count], src_w_ref[...], dot_t)
    receiver_sum = wide_dot(sums[7 * count :], dst_w_ref[...], dot_t)
    grad = upstreams[2 * count :] + receiver_sum + sender_sum
    grad_ref[...] = grad
    _, normed, inv_std = layer_norm(enc_agg_ref[...], enc_gain_ref[...])
    rows = norm_back(normed, inv_std, enc_gain_ref[...], grad)
    times = tiled_ref.shape[0] // count
    tiled_ref[...] = jnp.concatenate([rows] * times, axis=0).astype(BF16)


def mesh_kernel(tiled_ref, slopes_ref, grad_ref, out_w_ref, dst_w_ref, out_ref):
    count = grad_ref.shape[0]
    rows = dot_t(tiled_ref[: 2 * count, :], out_w_ref[...])[:count]
    out_ref[...] = (
        grad_ref[...] + wide_dot(rows * slopes_ref[...], dst_w_ref[...], dot_t)
    ).astype(BF16)


def mate_kernel(
    grad_ref, dst_ref, pick_t_ref, slope_ref, out_w_ref, src_w_ref, table_ref, part_ref, buf, sems
):
    half = dst_ref.shape[0] // 2
    (arriving,) = row_copies(slope_ref, buf, sems, half, half)
    arriving.start()
    table = stack_split(dot_t(grad_ref[...], out_w_ref[...]))
    table_ref[...] = table
    spread = spread_rows(dst_ref[half:, :], table)
    arriving.wait()
    edge = (spread * buf[...].astype(F32)).astype(BF16)
    part_ref[...] = wide_dot(dot(pick_t_ref[:, half:], edge), src_w_ref[...], dot_t).astype(BF16)


def own_kernel(table_ref, dst_ref, pick_t_ref, slope_ref, src_w_ref, part_ref, buf, sems):
    half = dst_ref.shape[0] // 2
    (arriving,) = row_copies(slope_ref, buf, sems, half)
    arriving.start()
    spread = spread_rows(dst_ref[:half, :], table_ref[...])
    arriving.wait()
    edge = (spread * buf[...].astype(F32)).astype(BF16)
    part_ref[...] = wide_dot(dot(pick_t_ref[:, :half], edge), src_w_ref[...], dot_t)


def join_kernel(own_ref, mate_ref, out_ref):
    out_ref[...] = (own_ref[...] + mate_ref[...].astype(F32)).astype(BF16)


def per_device(
    grid_latent,
    mesh_latent,
    g2m_src,
    g2m_peer,
    g2m_slot,
    proc_src,
    proc_dst,
    enc_src_w,
    enc_dst_w,
    enc_out_w,
    enc_bias,
    enc_gain,
    proc_src_w,
    proc_dst_w,
    proc_out_w,
    proc_bias,
    proc_gain,
    cotangent,
):
    feats = lax.axis_size("feat")
    bands = lax.axis_size("band")
    chips = feats // 2
    core = lax.axis_index("feat") % 2
    band = lax.axis_index("band")
    edges = g2m_src.shape[0]
    grids, latent = grid_latent.shape
    nodes = mesh_latent.shape[0]
    plane_nodes = chips * nodes
    plane = [[2 * chip + side for chip in range(chips)] for side in range(2)]
    shape = jax.ShapeDtypeStruct
    row = lambda vector: vector.reshape(1, latent)
    sem = lambda count: pltpu.SemaphoreType.DMA((count,))
    edge_buf = lambda count, kind: pltpu.VMEM((count, latent), kind)

    def exchange(values):
        return lax.all_to_all(
            values.reshape(chips, nodes, -1), "feat", split_axis=0, concat_axis=0, tiled=True,
            axis_index_groups=plane,
        )

    def swap(values):
        return lax.ppermute(values, "feat", [(i, i ^ 1) for i in range(feats)])

    far_side = lambda step: [
        pair
        for i in range(bands - step)
        if i & step
        for pair in ((i, i + step), (i + step, i))
    ]
    near_side = lambda step: [(i, i ^ step) for i in range(bands)]
    line = lambda index: index.reshape(1, edges)

    tiled_mesh = call(
        tile_kernel, shape((chips, nodes, latent), BF16), mesh_latent,
        far=(0,), far_out=(0,), scratch=(sem(chips),),
    )
    pack, near = call(
        prep_kernel,
        (shape((grids + 16, latent), BF16), shape((2 * nodes, latent), BF16)),
        grid_latent, cotangent, line(g2m_src), line(g2m_peer), line(g2m_slot),
        proc_src.reshape(1, -1), proc_dst.reshape(1, -1),
        far=range(7), far_out=(0,), cost=0,
        scratch=(
            edge_buf(nodes, BF16),
            pltpu.VMEM((3, 1, edges), jnp.int32),
            pltpu.VMEM((1, latent), jnp.int32),
            edge_buf(16, BF16),
            sem(8),
        ),
    )
    packs = lax.all_gather(
        pack, "feat", axis=0, tiled=True, axis_index_groups=[[i, i + 1] for i in range(0, feats, 2)]
    )
    mate_pack = lax.dynamic_slice_in_dim(packs, (1 - core) * pack.shape[0], pack.shape[0])
    mesh_all = exchange(tiled_mesh).reshape(plane_nodes, latent)

    mate_index = mate_pack[grids : grids + 3].astype(jnp.int32)
    joined = lambda own, place: jnp.concatenate([own, mate_index[place]])
    source, peer, slot = joined(g2m_src, 0), joined(g2m_peer[:, 0], 1), joined(g2m_slot, 2)
    target = jnp.where(peer % 2 == core, peer // 2 * nodes + slot, -1)
    grid_ids = jnp.arange(grids, dtype=jnp.int32)
    node_ids = jnp.arange(plane_nodes, dtype=jnp.int32)
    src_pick = (source[:, None] == grid_ids[None, :]).astype(BF16)
    src_pick_t = (source[None, :] == grid_ids[:, None]).astype(BF16)
    dst_pick = (target[:, None] == node_ids[None, :]).astype(BF16)

    step_one = jnp.where(band & 1 == 0, 1, -1)
    step_two = jnp.where(band & 2 == 0, 2, -2)
    inside = lambda place: jnp.logical_and(place >= 0, place < bands)
    info = jnp.stack([step_one, step_two, inside(band + step_one), inside(band - step_one)])

    pre_src = call(
        src_kernel, shape((2 * edges, latent), F32),
        grid_latent, mate_pack, src_pick, enc_src_w, row(enc_bias),
        far_out=(0,), scratch=(edge_buf(2 * edges, F32), sem(4)), cost=0,
    )
    partial, slope = call(
        enc_kernel,
        (shape((plane_nodes, 2 * latent), BF16), shape((2 * edges, latent), BF16)),
        pre_src, dst_pick, mesh_all, enc_dst_w,
        far=(0,), far_out=(0, 1),
        scratch=(
            edge_buf(2 * edges, F32), edge_buf(2 * edges, BF16), edge_buf(2 * edges, BF16),
            pltpu.VMEM((plane_nodes, 2 * latent), BF16), sem(8), sem(1), sem(2),
        ),
    )
    mid, packet, enc_agg, slopes = call(
        mid_kernel,
        (
            shape((nodes, latent), BF16),
            shape((3 * nodes, latent), BF16),
            shape((nodes, latent), F32),
            shape((nodes, latent), F32),
        ),
        exchange(partial), enc_out_w, row(enc_gain), mesh_latent, near,
    )
    mesh_out, grad_mid, tiled = call(
        proc_kernel,
        (
            shape((nodes, latent), BF16),
            shape((nodes, latent), F32),
            shape((plane_nodes, latent), BF16),
        ),
        lax.ppermute(packet, "band", near_side(1)),
        lax.ppermute(packet, "band", far_side(1)),
        lax.ppermute(mid, "band", near_side(2)),
        lax.ppermute(mid, "band", far_side(2)),
        packet, info.astype(jnp.int32), proc_src_w, proc_dst_w, proc_out_w, row(proc_bias),
        row(proc_gain), enc_agg, row(enc_gain),
        small=(5,),
    )
    grad_all = exchange(tiled).reshape(plane_nodes, latent)
    grad_mesh = call(
        mesh_kernel, shape((nodes, latent), BF16), tiled, slopes, grad_mid, enc_out_w, enc_dst_w,
    )
    table, mate_grad = call(
        mate_kernel, (shape((2 * plane_nodes, latent), BF16), shape((grids, latent), BF16)),
        grad_all, dst_pick, src_pick_t, slope, enc_out_w, enc_src_w,
        far=(3,), scratch=(edge_buf(edges, BF16), sem(1)),
    )
    own_grad = call(
        own_kernel, shape((grids, latent), F32), table, dst_pick, src_pick_t, slope, enc_src_w,
        far=(3,), scratch=(edge_buf(edges, BF16), sem(1)),
    )
    grad_grid = call(join_kernel, shape((grids, latent), BF16), own_grad, swap(mate_grad))
    return (mesh_out, grad_grid, grad_mesh)


def solution(mesh):
    shard = ("band", "feat")
    placed = (P(shard, None), P(shard, None), P(shard), P(shard, None), P(shard), P(shard), P(shard))
    placed += (P(),) * 10 + (P(shard, None),)
    return jax.shard_map(
        per_device,
        mesh=mesh,
        in_specs=placed,
        out_specs=(P(shard, None), P(shard, None), P(shard, None)),
        check_vma=False,
    )
```

```python
import jax
import jax.numpy as jnp
from jax import lax
from jax.experimental import pallas as pl
from jax.experimental.pallas import tpu as pltpu
from jax.sharding import PartitionSpec as P

BF16 = jnp.bfloat16
F32 = jnp.float32


def dot(left, right):
    return jnp.dot(left, right, preferred_element_type=F32)


def dot_t(left, right):
    return lax.dot_general(left, right, (((1,), (1,)), ((), ())), preferred_element_type=F32)


def split(values):
    high = values.astype(BF16)
    return high, (values - high.astype(F32)).astype(BF16)


def wide_dot(values, weight, product):
    rows = values.shape[0]
    high, low = split(values)
    both = product(jnp.concatenate([high.astype(F32), low.astype(F32)], axis=0).astype(BF16), weight)
    return both[:rows] + both[rows:]


def thirds(values):
    high, rest = values.astype(BF16), values
    rest = rest - high.astype(F32)
    mid = rest.astype(BF16).astype(F32)
    low = (rest - mid).astype(BF16).astype(F32)
    return jnp.concatenate([high.astype(F32), mid, low], axis=0).astype(BF16)


def layer_norm(values, gain):
    average = jnp.mean(values, axis=-1, keepdims=True)
    centred = values - average
    spread = jnp.mean(centred * centred, axis=-1, keepdims=True)
    inv_std = lax.rsqrt(spread + 1e-05)
    normed = centred * inv_std
    return normed * gain, normed, inv_std


def norm_back(normed, inv_std, gain, upstream):
    scaled = upstream * gain
    return inv_std * (
        scaled
        - jnp.mean(scaled, axis=-1, keepdims=True)
        - normed * jnp.mean(scaled * normed, axis=-1, keepdims=True)
    )


def call(body, out, *args, far=(), far_out=(), small=(), scratch=(), limit=16, cost=1):
    place = lambda there: pl.BlockSpec(memory_space=pltpu.HBM if there else pltpu.VMEM)
    single = not isinstance(out, tuple)
    outs = (out,) if single else out
    out_specs = tuple(place(i in far_out) for i in range(len(outs)))
    outs = tuple(
        pltpu.HBM(one.shape, one.dtype) if i in far_out else one for i, one in enumerate(outs)
    )
    args = tuple(
        pltpu.with_memory_space_constraint(arg, pltpu.HBM) if i in far else arg
        for i, arg in enumerate(args)
    )
    return pl.pallas_call(
        body,
        out_shape=outs[0] if single else outs,
        in_specs=[
            pl.BlockSpec(memory_space=pltpu.SMEM) if i in small else place(i in far)
            for i in range(len(args))
        ],
        out_specs=out_specs[0] if single else out_specs,
        scratch_shapes=scratch,
        compiler_params=pltpu.CompilerParams(vmem_limit_bytes=limit * 2**20 or None),
        cost_estimate=pl.CostEstimate(
            flops=cost * 4 * 10**9, bytes_accessed=cost * 2**22, transcendentals=0
        ),
    )(*args)


def dot_first(left, right):
    return lax.dot_general(left, right, (((0,), (0,)), ((), ())), preferred_element_type=F32)


def row_copies(source, target, sems, tile, offset=0):
    return [
        pltpu.make_async_copy(
            source.at[offset + i * tile : offset + (i + 1) * tile, :],
            target.at[i * tile : (i + 1) * tile, :],
            sems.at[i],
        )
        for i in range(sems.shape[0])
    ]


def silu_parts(values):
    sigma = 0.5 + 0.5 * jnp.tanh(0.5 * values)
    hidden = values * sigma
    return hidden.astype(BF16), sigma * (1.0 + (values - hidden))


def tile_kernel(mesh_ref, tiled_ref, buf, sem):
    copy = pltpu.make_async_copy(mesh_ref, buf, sem.at[0])
    copy.start()
    copy.wait()
    times = tiled_ref.shape[0] // buf.shape[0]
    tiled_ref[...] = jnp.concatenate([buf[...].astype(F32)] * times, axis=0).astype(BF16)


def prep_kernel(
    grid_ref, cotangent_ref, src_ref, peer_ref, slot_ref, sender_ref, receiver_ref,
    pack_ref, near_ref, cotangent_buf, index_buf, near_buf, sems,
):
    count, latent = cotangent_buf.shape
    grids = grid_ref.shape[0]
    half = sender_ref.shape[1]
    pairs = (
        (src_ref, index_buf.at[0]),
        (peer_ref, index_buf.at[1]),
        (slot_ref, index_buf.at[2]),
        (sender_ref, near_buf.at[:, :half]),
        (receiver_ref, near_buf.at[:, half:]),
        (cotangent_ref, cotangent_buf),
        (grid_ref, pack_ref.at[:grids, :]),
    )
    copies = [pltpu.make_async_copy(*pair, sems.at[i]) for i, pair in enumerate(pairs)]
    for copy in copies:
        copy.start()
    for copy in copies[:6]:
        copy.wait()
    spare = pack_ref.shape[0] - grids
    place = lax.broadcasted_iota(jnp.int32, (spare, latent), 0)
    index = jnp.where(place == 0, index_buf[0], jnp.where(place == 1, index_buf[1], index_buf[2]))
    pack_ref[grids:, :] = index.astype(F32).astype(BF16)
    ends = jnp.broadcast_to(near_buf[...], (count, 2 * half)).astype(F32)
    near_ref[...] = jnp.concatenate([cotangent_buf[...].astype(F32), ends], axis=0).astype(BF16)
    copies[6].wait()


def src_kernel(own_ref, mate_ref, pick_ref, rows_ref):
    tile = own_ref.shape[0]
    edges = pick_ref.shape[0]
    for start in range(0, edges, tile):
        grid_ref = own_ref if start < edges // 2 else mate_ref
        picked = dot(pick_ref[start : start + tile, :], grid_ref[:tile, :])
        rows_ref[start : start + tile, :] = picked.astype(BF16)


def stack_split(values):
    high = values.astype(BF16).astype(F32)
    return jnp.concatenate([high, values - high], axis=0).astype(BF16)


def spread_rows(pick, table):
    half = table.shape[0] // 2
    return dot(pick, table[:half]) + dot(pick, table[half:])


def enc_kernel(
    rows_ref, dst_ref, dst_t_ref, mesh_ref, src_w_ref, dst_w_ref, bias_ref, sum_ref, slope_ref,
    both, slope_buf, sems,
):
    latent = dst_w_ref.shape[1]
    tile = slope_buf.shape[0] // sems.shape[0]
    leaving = row_copies(slope_buf, slope_ref, sems, tile)
    table = stack_split(dot(mesh_ref[...], dst_w_ref[...]) + bias_ref[...])
    for i, copy in enumerate(leaving):
        rows = slice(i * tile, (i + 1) * tile)
        spread = spread_rows(dst_ref[rows, :], table)
        hidden, slope = silu_parts(dot(rows_ref[rows, :], src_w_ref[...]) + spread)
        both[rows, :latent] = hidden
        both[rows, latent:] = slope.astype(BF16)
        slope_buf[rows, :] = slope.astype(BF16)
        copy.start()
    total = dot(dst_t_ref[...], both[...])
    nodes = sum_ref.shape[1] // 2
    chunked = lambda v: v.reshape(-1, nodes, latent)
    sum_ref[...] = jnp.concatenate(
        [chunked(total[:, :latent]), chunked(total[:, latent:])], axis=1
    ).astype(BF16)
    for copy in leaving:
        copy.wait()


def mid_kernel(
    parts_ref, weight_ref, gain_ref, mesh_ref, near_ref, mid_ref, packet_ref, agg_ref, slopes_ref
):
    count = mesh_ref.shape[0]
    summed = jnp.sum(parts_ref[...].astype(F32), axis=0)
    agg = wide_dot(summed[:count], weight_ref[...], dot)
    slopes_ref[...] = summed[count:]
    agg_ref[...] = agg
    mid = mesh_ref[...].astype(F32) + layer_norm(agg, gain_ref[...])[0]
    mid_ref[...] = mid.astype(BF16)
    packet_ref[...] = jnp.concatenate([mid, near_ref[...].astype(F32)], axis=0).astype(BF16)


def edge_ends(index, info_ref, offset, inside, group, count):
    half = index.shape[1] // 2
    source, receiver = index[:, :half], index[:, half:]
    bits = count.bit_length() - 1
    shift = offset + jnp.right_shift(source, bits) - 1
    one, two = info_ref[0], info_ref[1]
    spot = jnp.where(
        shift == 0, 4,
        jnp.where(
            shift == one, 0, jnp.where(shift == -one, 1, jnp.where(shift == two, 2, 3))
        ),
    )
    keep = lambda column: column * inside + (inside - 1)
    return (
        keep(spot * count + jnp.bitwise_and(source, count - 1)),
        keep((5 + group) * count + receiver),
    )


def partner_rows(ref, first, valid):
    rows = ref[...].astype(F32)
    half = rows.shape[0] // 2
    return jnp.where(first == 0, rows[half:], rows[:half]) * valid.astype(F32)


def proc_kernel(
    one_ref, two_ref, three_ref, four_ref, own_ref, info_ref, src_w_ref, dst_w_ref, out_w_ref,
    bias_ref, gain_ref, enc_agg_ref, enc_gain_ref, out_ref, grad_ref, tiled_ref,
):
    count = out_ref.shape[0]
    packets = [
        partner_rows(one_ref, info_ref[4], info_ref[2]),
        partner_rows(two_ref, 1 - info_ref[4], info_ref[3]),
        own_ref[...].astype(F32),
    ]
    three = partner_rows(three_ref, info_ref[5], info_ref[6])
    four = partner_rows(four_ref, 1 - info_ref[5], info_ref[7])
    one, two, mid = (packet[:count] for packet in packets)
    upstreams = jnp.concatenate([packet[count : 2 * count] for packet in packets], axis=0)
    index = [packet[2 * count : 2 * count + 1].astype(jnp.int32) for packet in packets]
    step = info_ref[0]
    columns = [
        edge_ends(index[0], info_ref, step, info_ref[2], 0, count),
        edge_ends(index[1], info_ref, -step, info_ref[3], 1, count),
        edge_ends(index[2], info_ref, 0, 1, 2, count),
    ]
    sender, receiver = (jnp.concatenate(column, axis=1) for column in zip(*columns))
    ids = lax.broadcasted_iota(jnp.int32, (8 * count, sender.shape[1]), 0)
    chosen = jnp.where(jnp.logical_or(ids == sender, ids == receiver), 1.0, 0.0)
    pick_t = chosen.astype(BF16)
    pick = jnp.concatenate([chosen] * 3, axis=0).astype(BF16)

    rows = [one, two, three, four, mid]
    senders = jnp.concatenate(rows, axis=0).astype(BF16)
    receivers = jnp.concatenate([one, two, mid], axis=0).astype(BF16)
    table = jnp.concatenate(
        [dot(senders, src_w_ref[...]), dot(receivers, dst_w_ref[...]) + bias_ref[...]], axis=0
    )
    hidden, slope = silu_parts(dot_first(pick, thirds(table)))
    summed = dot(pick_t, hidden)[5 * count :]
    agg = wide_dot(summed, out_w_ref[...], dot)
    shifted, normed, inv_std = layer_norm(agg, gain_ref[...])
    out_ref[...] = (mid + shifted[2 * count :]).astype(BF16)
    grad_agg = norm_back(normed, inv_std, gain_ref[...], upstreams).astype(BF16)
    back = dot_t(grad_agg, out_w_ref[...])
    blank = jnp.zeros((5 * count, back.shape[1]), F32)
    spread = dot_first(pick, thirds(jnp.concatenate([blank, back], axis=0)))
    sums = dot(pick_t, (spread * slope).astype(BF16))
    sender_sum = wide_dot(sums[4 * count : 5 * count], src_w_ref[...], dot_t)
    receiver_sum = wide_dot(sums[7 * count :], dst_w_ref[...], dot_t)
    grad = upstreams[2 * count :] + receiver_sum + sender_sum
    grad_ref[...] = grad
    _, normed, inv_std = layer_norm(enc_agg_ref[...], enc_gain_ref[...])
    rows = norm_back(normed, inv_std, enc_gain_ref[...], grad)
    times = tiled_ref.shape[0] // count
    tiled_ref[...] = jnp.concatenate([rows] * times, axis=0).astype(BF16)


def mesh_kernel(tiled_ref, slopes_ref, grad_ref, out_w_ref, dst_w_ref, out_ref):
    count = grad_ref.shape[0]
    rows = dot_t(tiled_ref[: 2 * count, :], out_w_ref[...])[:count]
    out_ref[...] = (
        grad_ref[...] + wide_dot(rows * slopes_ref[...], dst_w_ref[...], dot_t)
    ).astype(BF16)


def mate_kernel(
    grad_ref, dst_ref, pick_t_ref, slope_ref, out_w_ref, src_w_ref, table_ref, part_ref, buf, sems
):
    half = dst_ref.shape[0] // 2
    (arriving,) = row_copies(slope_ref, buf, sems, half, half)
    arriving.start()
    table = stack_split(dot_t(grad_ref[...], out_w_ref[...]))
    table_ref[...] = table
    spread = spread_rows(dst_ref[half:, :], table)
    arriving.wait()
    edge = (spread * buf[...].astype(F32)).astype(BF16)
    part_ref[...] = wide_dot(dot(pick_t_ref[:, half:], edge), src_w_ref[...], dot_t).astype(BF16)


def own_kernel(table_ref, dst_ref, pick_t_ref, slope_ref, src_w_ref, part_ref, buf, sems):
    half = dst_ref.shape[0] // 2
    (arriving,) = row_copies(slope_ref, buf, sems, half)
    arriving.start()
    spread = spread_rows(dst_ref[:half, :], table_ref[...])
    arriving.wait()
    edge = (spread * buf[...].astype(F32)).astype(BF16)
    part_ref[...] = wide_dot(dot(pick_t_ref[:, :half], edge), src_w_ref[...], dot_t)


def join_kernel(own_ref, mate_ref, out_ref):
    out_ref[...] = (own_ref[...] + mate_ref[...].astype(F32)).astype(BF16)


def per_device(
    grid_latent,
    mesh_latent,
    g2m_src,
    g2m_peer,
    g2m_slot,
    proc_src,
    proc_dst,
    enc_src_w,
    enc_dst_w,
    enc_out_w,
    enc_bias,
    enc_gain,
    proc_src_w,
    proc_dst_w,
    proc_out_w,
    proc_bias,
    proc_gain,
    cotangent,
):
    feats = lax.axis_size("feat")
    bands = lax.axis_size("band")
    chips = feats // 2
    core = lax.axis_index("feat") % 2
    band = lax.axis_index("band")
    edges = g2m_src.shape[0]
    grids, latent = grid_latent.shape
    nodes = mesh_latent.shape[0]
    plane_nodes = chips * nodes
    plane = [[2 * chip + side for chip in range(chips)] for side in range(2)]
    shape = jax.ShapeDtypeStruct
    row = lambda vector: vector.reshape(1, latent)
    sem = lambda count: pltpu.SemaphoreType.DMA((count,))
    edge_buf = lambda count, kind: pltpu.VMEM((count, latent), kind)

    def exchange(values):
        return lax.all_to_all(
            values.reshape(chips, -1, latent), "feat", split_axis=0, concat_axis=0, tiled=True,
            axis_index_groups=plane,
        )

    def swap(values):
        return lax.ppermute(values, "feat", [(i, i ^ 1) for i in range(feats)])

    near_side = lambda step: [[i, i + step] for i in range(bands) if not i & step]
    far_side = lambda step: [[i, (i + step) % bands] for i in range(bands) if i & step]

    def meet(values, groups):
        return lax.all_gather(values, "band", axis=0, tiled=True, axis_index_groups=groups)

    line = lambda index: index.reshape(1, edges)

    tiled_mesh = call(
        tile_kernel, shape((plane_nodes, latent), BF16), mesh_latent,
        far=(0,), scratch=(edge_buf(nodes, BF16), sem(1)),
    )
    pack, near = call(
        prep_kernel,
        (shape((grids + 16, latent), BF16), shape((2 * nodes, latent), BF16)),
        grid_latent, cotangent, line(g2m_src), line(g2m_peer), line(g2m_slot),
        proc_src.reshape(1, -1), proc_dst.reshape(1, -1),
        far=range(7), cost=0,
        scratch=(
            edge_buf(nodes, BF16),
            pltpu.VMEM((3, 1, edges), jnp.int32),
            pltpu.VMEM((1, latent), jnp.int32),
            sem(7),
        ),
    )
    packs = lax.all_gather(
        pack, "feat", axis=0, tiled=True, axis_index_groups=[[i, i + 1] for i in range(0, feats, 2)]
    )
    mate_pack = lax.dynamic_slice_in_dim(packs, (1 - core) * pack.shape[0], pack.shape[0])
    mesh_all = exchange(tiled_mesh).reshape(plane_nodes, latent)

    mate_index = mate_pack[grids : grids + 3].astype(jnp.int32)
    joined = lambda own, place: jnp.concatenate([own, mate_index[place]])
    source, peer, slot = joined(g2m_src, 0), joined(g2m_peer[:, 0], 1), joined(g2m_slot, 2)
    target = jnp.where(peer % 2 == core, peer // 2 * nodes + slot, -1)
    grid_ids = jnp.arange(grids, dtype=jnp.int32)
    node_ids = jnp.arange(plane_nodes, dtype=jnp.int32)
    src_pick = (source[:, None] == grid_ids[None, :]).astype(BF16)
    src_pick_t = (source[None, :] == grid_ids[:, None]).astype(BF16)
    dst_pick = (target[:, None] == node_ids[None, :]).astype(BF16)
    dst_pick_t = (target[None, :] == node_ids[:, None]).astype(BF16)

    step_one = jnp.where(band & 1 == 0, 1, -1)
    step_two = jnp.where(band & 2 == 0, 2, -2)
    inside = lambda place: jnp.logical_and(place >= 0, place < bands)
    info = jnp.stack([
        step_one, step_two, inside(band + step_one), inside(band - step_one),
        band & 1, (band & 2) // 2, inside(band + step_two), inside(band - step_two),
    ])

    src_rows = call(
        src_kernel, shape((2 * edges, latent), BF16), grid_latent, mate_pack, src_pick, cost=0,
    )
    partial, slope = call(
        enc_kernel,
        (shape((chips, 2 * nodes, latent), BF16), shape((2 * edges, latent), BF16)),
        src_rows, dst_pick, dst_pick_t, mesh_all, enc_src_w, enc_dst_w, row(enc_bias),
        far_out=(1,),
        scratch=(pltpu.VMEM((2 * edges, 2 * latent), BF16), edge_buf(2 * edges, BF16), sem(4)),
    )
    mid, packet, enc_agg, slopes = call(
        mid_kernel,
        (
            shape((nodes, latent), BF16),
            shape((3 * nodes, latent), BF16),
            shape((nodes, latent), F32),
            shape((nodes, latent), F32),
        ),
        exchange(partial), enc_out_w, row(enc_gain), mesh_latent, near,
    )
    mesh_out, grad_mid, tiled = call(
        proc_kernel,
        (
            shape((nodes, latent), BF16),
            shape((nodes, latent), F32),
            shape((plane_nodes, latent), BF16),
        ),
        meet(packet, near_side(1)), meet(packet, far_side(1)),
        meet(mid, near_side(2)), meet(mid, far_side(2)),
        packet, info.astype(jnp.int32), proc_src_w, proc_dst_w, proc_out_w, row(proc_bias),
        row(proc_gain), enc_agg, row(enc_gain),
        small=(5,),
    )
    grad_all = exchange(tiled).reshape(plane_nodes, latent)
    grad_mesh = call(
        mesh_kernel, shape((nodes, latent), BF16), tiled, slopes, grad_mid, enc_out_w, enc_dst_w,
    )
    table, mate_grad = call(
        mate_kernel, (shape((2 * plane_nodes, latent), BF16), shape((grids, latent), BF16)),
        grad_all, dst_pick, src_pick_t, slope, enc_out_w, enc_src_w,
        far=(3,), scratch=(edge_buf(edges, BF16), sem(1)),
    )
    own_grad = call(
        own_kernel, shape((grids, latent), F32), table, dst_pick, src_pick_t, slope, enc_src_w,
        far=(3,), scratch=(edge_buf(edges, BF16), sem(1)),
    )
    grad_grid = call(join_kernel, shape((grids, latent), BF16), own_grad, swap(mate_grad))
    return (mesh_out, grad_grid, grad_mesh)


def solution(mesh):
    shard = ("band", "feat")
    placed = (P(shard, None), P(shard, None), P(shard), P(shard, None), P(shard), P(shard), P(shard))
    placed += (P(),) * 10 + (P(shard, None),)
    return jax.shard_map(
        per_device,
        mesh=mesh,
        in_specs=placed,
        out_specs=(P(shard, None), P(shard, None), P(shard, None)),
        check_vma=False,
    )
```

```python
import jax
import jax.numpy as jnp
from jax import lax
from jax.experimental import pallas as pl
from jax.experimental.pallas import tpu as pltpu
from jax.sharding import PartitionSpec as P

BF16 = jnp.bfloat16
F32 = jnp.float32


def dot(left, right):
    return jnp.dot(left, right, preferred_element_type=F32)


def dot_t(left, right):
    return lax.dot_general(left, right, (((1,), (1,)), ((), ())), preferred_element_type=F32)


def split(values):
    high = values.astype(BF16)
    return high, (values - high.astype(F32)).astype(BF16)


def wide_dot(values, weight, product):
    rows = values.shape[0]
    high, low = split(values)
    both = product(jnp.concatenate([high.astype(F32), low.astype(F32)], axis=0).astype(BF16), weight)
    return both[:rows] + both[rows:]


def layer_norm(values, gain):
    average = jnp.mean(values, axis=-1, keepdims=True)
    centred = values - average
    spread = jnp.mean(centred * centred, axis=-1, keepdims=True)
    inv_std = lax.rsqrt(spread + 1e-05)
    normed = centred * inv_std
    return normed * gain, normed, inv_std


def norm_back(normed, inv_std, gain, upstream):
    scaled = upstream * gain
    return inv_std * (
        scaled
        - jnp.mean(scaled, axis=-1, keepdims=True)
        - normed * jnp.mean(scaled * normed, axis=-1, keepdims=True)
    )


def call(body, out, *args, far=(), far_out=(), small=(), scratch=(), limit=16, cost=1):
    place = lambda there: pl.BlockSpec(memory_space=pltpu.HBM if there else pltpu.VMEM)
    single = not isinstance(out, tuple)
    outs = (out,) if single else out
    out_specs = tuple(place(i in far_out) for i in range(len(outs)))
    outs = tuple(
        pltpu.HBM(one.shape, one.dtype) if i in far_out else one for i, one in enumerate(outs)
    )
    args = tuple(
        pltpu.with_memory_space_constraint(arg, pltpu.HBM) if i in far else arg
        for i, arg in enumerate(args)
    )
    return pl.pallas_call(
        body,
        out_shape=outs[0] if single else outs,
        in_specs=[
            pl.BlockSpec(memory_space=pltpu.SMEM) if i in small else place(i in far)
            for i in range(len(args))
        ],
        out_specs=out_specs[0] if single else out_specs,
        scratch_shapes=scratch,
        compiler_params=pltpu.CompilerParams(vmem_limit_bytes=limit * 2**20 or None),
        cost_estimate=pl.CostEstimate(
            flops=cost * 4 * 10**9, bytes_accessed=cost * 2**22, transcendentals=0
        ),
    )(*args)


def dot_first(left, right):
    return lax.dot_general(left, right, (((0,), (0,)), ((), ())), preferred_element_type=F32)


def row_copies(source, target, sems, tile, offset=0):
    return [
        pltpu.make_async_copy(
            source.at[offset + i * tile : offset + (i + 1) * tile, :],
            target.at[i * tile : (i + 1) * tile, :],
            sems.at[i],
        )
        for i in range(sems.shape[0])
    ]


def silu_parts(values):
    sigma = 0.5 + 0.5 * jnp.tanh(0.5 * values)
    hidden = values * sigma
    return hidden.astype(BF16), sigma * (1.0 + (values - hidden))


def tile_kernel(mesh_ref, tiled_ref, buf, sem):
    copy = pltpu.make_async_copy(mesh_ref, buf, sem.at[0])
    copy.start()
    copy.wait()
    times = tiled_ref.shape[0] // buf.shape[0]
    tiled_ref[...] = jnp.concatenate([buf[...].astype(F32)] * times, axis=0).astype(BF16)


def prep_kernel(
    grid_ref, cotangent_ref, src_ref, peer_ref, slot_ref, sender_ref, receiver_ref,
    pack_ref, near_ref, cotangent_buf, index_buf, near_buf, sems,
):
    count, latent = cotangent_buf.shape
    grids = grid_ref.shape[0]
    half = sender_ref.shape[1]
    pairs = (
        (src_ref, index_buf.at[0]),
        (peer_ref, index_buf.at[1]),
        (slot_ref, index_buf.at[2]),
        (sender_ref, near_buf.at[:, :half]),
        (receiver_ref, near_buf.at[:, half:]),
        (cotangent_ref, cotangent_buf),
        (grid_ref, pack_ref.at[:grids, :]),
    )
    copies = [pltpu.make_async_copy(*pair, sems.at[i]) for i, pair in enumerate(pairs)]
    for copy in copies:
        copy.start()
    for copy in copies[:6]:
        copy.wait()
    spare = pack_ref.shape[0] - grids
    place = lax.broadcasted_iota(jnp.int32, (spare, latent), 0)
    index = jnp.where(place == 0, index_buf[0], jnp.where(place == 1, index_buf[1], index_buf[2]))
    pack_ref[grids:, :] = index.astype(F32).astype(BF16)
    ends = jnp.broadcast_to(near_buf[...], (count, 2 * half)).astype(F32)
    near_ref[...] = jnp.concatenate([cotangent_buf[...].astype(F32), ends], axis=0).astype(BF16)
    copies[6].wait()


def src_kernel(own_ref, mate_ref, pick_ref, rows_ref):
    tile = own_ref.shape[0]
    edges = pick_ref.shape[0]
    for start in range(0, edges, tile):
        grid_ref = own_ref if start < edges // 2 else mate_ref
        picked = dot(pick_ref[start : start + tile, :], grid_ref[:tile, :])
        rows_ref[start : start + tile, :] = picked.astype(BF16)


def stack_split(values):
    high = values.astype(BF16).astype(F32)
    return jnp.concatenate([high, values - high], axis=0).astype(BF16)


def spread_rows(pick, table):
    half = table.shape[0] // 2
    return dot(pick, table[:half]) + dot(pick, table[half:])


def enc_kernel(
    rows_ref, dst_ref, dst_t_ref, mesh_ref, src_w_ref, dst_w_ref, bias_ref, sum_ref, slope_ref,
    both, slope_buf, sems,
):
    latent = dst_w_ref.shape[1]
    tile = slope_buf.shape[0] // sems.shape[0]
    leaving = row_copies(slope_buf, slope_ref, sems, tile)
    table = stack_split(dot(mesh_ref[...], dst_w_ref[...]) + bias_ref[...])
    for i, copy in enumerate(leaving):
        rows = slice(i * tile, (i + 1) * tile)
        spread = spread_rows(dst_ref[rows, :], table)
        hidden, slope = silu_parts(dot(rows_ref[rows, :], src_w_ref[...]) + spread)
        both[rows, :latent] = hidden
        both[rows, latent:] = slope.astype(BF16)
        slope_buf[rows, :] = slope.astype(BF16)
        copy.start()
    total = dot(dst_t_ref[...], both[...])
    nodes = sum_ref.shape[1] // 2
    chunked = lambda v: v.reshape(-1, nodes, latent)
    sum_ref[...] = jnp.concatenate(
        [chunked(total[:, :latent]), chunked(total[:, latent:])], axis=1
    ).astype(BF16)
    for copy in leaving:
        copy.wait()


def mid_kernel(
    parts_ref, weight_ref, gain_ref, mesh_ref, near_ref, mid_ref, packet_ref, agg_ref, slopes_ref
):
    count = mesh_ref.shape[0]
    summed = jnp.sum(parts_ref[...].astype(F32), axis=0)
    agg = wide_dot(summed[:count], weight_ref[...], dot)
    slopes_ref[...] = summed[count:]
    agg_ref[...] = agg
    mid = mesh_ref[...].astype(F32) + layer_norm(agg, gain_ref[...])[0]
    mid_ref[...] = mid.astype(BF16)
    packet_ref[...] = jnp.concatenate([mid, near_ref[...].astype(F32)], axis=0).astype(BF16)


def edge_ends(index, info_ref, offset, inside, group, count):
    half = index.shape[1] // 2
    source, receiver = index[:, :half], index[:, half:]
    bits = count.bit_length() - 1
    shift = offset + jnp.right_shift(source, bits) - 1
    one, two = info_ref[0], info_ref[1]
    spot = jnp.where(
        shift == 0, 4,
        jnp.where(
            shift == one, 0, jnp.where(shift == -one, 1, jnp.where(shift == two, 2, 3))
        ),
    )
    keep = lambda column: column * inside + (inside - 1)
    return (
        keep(spot * count + jnp.bitwise_and(source, count - 1)),
        keep((5 + group) * count + receiver),
    )


def proc_kernel(
    one_ref, two_ref, three_ref, four_ref, own_ref, info_ref, src_w_ref, dst_w_ref, out_w_ref,
    bias_ref, gain_ref, enc_agg_ref, enc_gain_ref, out_ref, grad_ref, tiled_ref,
):
    count = out_ref.shape[0]
    packets = [ref[...].astype(F32) for ref in (one_ref, two_ref, own_ref)]
    one, two, mid = (packet[:count] for packet in packets)
    upstreams = jnp.concatenate([packet[count : 2 * count] for packet in packets], axis=0)
    index = [packet[2 * count : 2 * count + 1].astype(jnp.int32) for packet in packets]
    step = info_ref[0]
    columns = [
        edge_ends(index[0], info_ref, step, info_ref[2], 0, count),
        edge_ends(index[1], info_ref, -step, info_ref[3], 1, count),
        edge_ends(index[2], info_ref, 0, 1, 2, count),
    ]
    sender, receiver = (jnp.concatenate(column, axis=1) for column in zip(*columns))
    ids = lax.broadcasted_iota(jnp.int32, (8 * count, sender.shape[1]), 0)
    chosen = jnp.where(jnp.logical_or(ids == sender, ids == receiver), 1.0, 0.0)
    pick_t = chosen.astype(BF16)
    pick = jnp.concatenate([chosen] * 2, axis=0).astype(BF16)

    rows = [one, two, three_ref[...].astype(F32), four_ref[...].astype(F32), mid]
    senders = jnp.concatenate(rows, axis=0).astype(BF16)
    receivers = jnp.concatenate([one, two, mid], axis=0).astype(BF16)
    table = jnp.concatenate(
        [dot(senders, src_w_ref[...]), dot(receivers, dst_w_ref[...]) + bias_ref[...]], axis=0
    )
    hidden, slope = silu_parts(dot_first(pick, stack_split(table)))
    summed = dot(pick_t, hidden)[5 * count :]
    agg = wide_dot(summed, out_w_ref[...], dot)
    shifted, normed, inv_std = layer_norm(agg, gain_ref[...])
    out_ref[...] = (mid + shifted[2 * count :]).astype(BF16)
    grad_agg = norm_back(normed, inv_std, gain_ref[...], upstreams).astype(BF16)
    back = dot_t(grad_agg, out_w_ref[...])
    blank = jnp.zeros((5 * count, back.shape[1]), F32)
    spread = dot_first(pick, stack_split(jnp.concatenate([blank, back], axis=0)))
    sums = dot(pick_t, (spread * slope).astype(BF16))
    sender_sum = wide_dot(sums[4 * count : 5 * count], src_w_ref[...], dot_t)
    receiver_sum = wide_dot(sums[7 * count :], dst_w_ref[...], dot_t)
    grad = upstreams[2 * count :] + receiver_sum + sender_sum
    grad_ref[...] = grad
    _, normed, inv_std = layer_norm(enc_agg_ref[...], enc_gain_ref[...])
    rows = norm_back(normed, inv_std, enc_gain_ref[...], grad)
    times = tiled_ref.shape[0] // count
    tiled_ref[...] = jnp.concatenate([rows] * times, axis=0).astype(BF16)


def mesh_kernel(tiled_ref, slopes_ref, grad_ref, out_w_ref, dst_w_ref, out_ref):
    count = grad_ref.shape[0]
    rows = dot_t(tiled_ref[: 2 * count, :], out_w_ref[...])[:count]
    out_ref[...] = (
        grad_ref[...] + wide_dot(rows * slopes_ref[...], dst_w_ref[...], dot_t)
    ).astype(BF16)


def mate_kernel(
    grad_ref, dst_ref, pick_t_ref, slope_ref, out_w_ref, src_w_ref, table_ref, part_ref, buf, sems
):
    half = dst_ref.shape[0] // 2
    (arriving,) = row_copies(slope_ref, buf, sems, half, half)
    arriving.start()
    table = stack_split(dot_t(grad_ref[...], out_w_ref[...]))
    table_ref[...] = table
    spread = spread_rows(dst_ref[half:, :], table)
    arriving.wait()
    edge = (spread * buf[...].astype(F32)).astype(BF16)
    part_ref[...] = wide_dot(dot(pick_t_ref[:, half:], edge), src_w_ref[...], dot_t).astype(BF16)


def own_kernel(table_ref, dst_ref, pick_t_ref, slope_ref, src_w_ref, part_ref, buf, sems):
    half = dst_ref.shape[0] // 2
    (arriving,) = row_copies(slope_ref, buf, sems, half)
    arriving.start()
    spread = spread_rows(dst_ref[:half, :], table_ref[...])
    arriving.wait()
    edge = (spread * buf[...].astype(F32)).astype(BF16)
    part_ref[...] = wide_dot(dot(pick_t_ref[:, :half], edge), src_w_ref[...], dot_t)


def join_kernel(own_ref, mate_ref, out_ref):
    out_ref[...] = (own_ref[...] + mate_ref[...].astype(F32)).astype(BF16)


def per_device(
    grid_latent,
    mesh_latent,
    g2m_src,
    g2m_peer,
    g2m_slot,
    proc_src,
    proc_dst,
    enc_src_w,
    enc_dst_w,
    enc_out_w,
    enc_bias,
    enc_gain,
    proc_src_w,
    proc_dst_w,
    proc_out_w,
    proc_bias,
    proc_gain,
    cotangent,
):
    feats = lax.axis_size("feat")
    bands = lax.axis_size("band")
    chips = feats // 2
    core = lax.axis_index("feat") % 2
    band = lax.axis_index("band")
    edges = g2m_src.shape[0]
    grids, latent = grid_latent.shape
    nodes = mesh_latent.shape[0]
    plane_nodes = chips * nodes
    plane = [[2 * chip + side for chip in range(chips)] for side in range(2)]
    shape = jax.ShapeDtypeStruct
    row = lambda vector: vector.reshape(1, latent)
    sem = lambda count: pltpu.SemaphoreType.DMA((count,))
    edge_buf = lambda count, kind: pltpu.VMEM((count, latent), kind)

    def exchange(values):
        return lax.all_to_all(
            values.reshape(chips, -1, latent), "feat", split_axis=0, concat_axis=0, tiled=True,
            axis_index_groups=plane,
        )

    def swap(values):
        return lax.ppermute(values, "feat", [(i, i ^ 1) for i in range(feats)])

    near_side = lambda step: [(i, i ^ step) for i in range(bands)]
    far_side = lambda step: [
        pair
        for i in range(bands - step)
        if i & step
        for pair in ((i, i + step), (i + step, i))
    ]

    def meet(values, pairs):
        return lax.ppermute(values, "band", pairs)

    line = lambda index: index.reshape(1, edges)

    tiled_mesh = call(
        tile_kernel, shape((plane_nodes, latent), BF16), mesh_latent,
        far=(0,), scratch=(edge_buf(nodes, BF16), sem(1)),
    )
    pack, near = call(
        prep_kernel,
        (shape((grids + 16, latent), BF16), shape((2 * nodes, latent), BF16)),
        grid_latent, cotangent, line(g2m_src), line(g2m_peer), line(g2m_slot),
        proc_src.reshape(1, -1), proc_dst.reshape(1, -1),
        far=range(7), cost=0,
        scratch=(
            edge_buf(nodes, BF16),
            pltpu.VMEM((3, 1, edges), jnp.int32),
            pltpu.VMEM((1, latent), jnp.int32),
            sem(7),
        ),
    )
    packs = lax.all_gather(
        pack, "feat", axis=0, tiled=True, axis_index_groups=[[i, i + 1] for i in range(0, feats, 2)]
    )
    mate_pack = lax.dynamic_slice_in_dim(packs, (1 - core) * pack.shape[0], pack.shape[0])
    mesh_all = exchange(tiled_mesh).reshape(plane_nodes, latent)

    mate_index = mate_pack[grids : grids + 3].astype(jnp.int32)
    joined = lambda own, place: jnp.concatenate([own, mate_index[place]])
    source, peer, slot = joined(g2m_src, 0), joined(g2m_peer[:, 0], 1), joined(g2m_slot, 2)
    target = jnp.where(peer % 2 == core, peer // 2 * nodes + slot, -1)
    grid_ids = jnp.arange(grids, dtype=jnp.int32)
    node_ids = jnp.arange(plane_nodes, dtype=jnp.int32)
    src_pick = (source[:, None] == grid_ids[None, :]).astype(BF16)
    src_pick_t = (source[None, :] == grid_ids[:, None]).astype(BF16)
    dst_pick = (target[:, None] == node_ids[None, :]).astype(BF16)
    dst_pick_t = (target[None, :] == node_ids[:, None]).astype(BF16)

    step_one = jnp.where(band & 1 == 0, 1, -1)
    step_two = jnp.where(band & 2 == 0, 2, -2)
    inside = lambda place: jnp.logical_and(place >= 0, place < bands)
    info = jnp.stack([step_one, step_two, inside(band + step_one), inside(band - step_one)])

    src_rows = call(
        src_kernel, shape((2 * edges, latent), BF16), grid_latent, mate_pack, src_pick, cost=0,
    )
    partial, slope = call(
        enc_kernel,
        (shape((chips, 2 * nodes, latent), BF16), shape((2 * edges, latent), BF16)),
        src_rows, dst_pick, dst_pick_t, mesh_all, enc_src_w, enc_dst_w, row(enc_bias),
        far_out=(1,),
        scratch=(pltpu.VMEM((2 * edges, 2 * latent), BF16), edge_buf(2 * edges, BF16), sem(4)),
    )
    mid, packet, enc_agg, slopes = call(
        mid_kernel,
        (
            shape((nodes, latent), BF16),
            shape((3 * nodes, latent), BF16),
            shape((nodes, latent), F32),
            shape((nodes, latent), F32),
        ),
        exchange(partial), enc_out_w, row(enc_gain), mesh_latent, near,
    )
    mesh_out, grad_mid, tiled = call(
        proc_kernel,
        (
            shape((nodes, latent), BF16),
            shape((nodes, latent), F32),
            shape((plane_nodes, latent), BF16),
        ),
        meet(packet, near_side(1)), meet(packet, far_side(1)),
        meet(mid, near_side(2)), meet(mid, far_side(2)),
        packet, info.astype(jnp.int32), proc_src_w, proc_dst_w, proc_out_w, row(proc_bias),
        row(proc_gain), enc_agg, row(enc_gain),
        small=(5,),
    )
    grad_all = exchange(tiled).reshape(plane_nodes, latent)
    grad_mesh = call(
        mesh_kernel, shape((nodes, latent), BF16), tiled, slopes, grad_mid, enc_out_w, enc_dst_w,
    )
    table, mate_grad = call(
        mate_kernel, (shape((2 * plane_nodes, latent), BF16), shape((grids, latent), BF16)),
        grad_all, dst_pick, src_pick_t, slope, enc_out_w, enc_src_w,
        far=(3,), scratch=(edge_buf(edges, BF16), sem(1)),
    )
    own_grad = call(
        own_kernel, shape((grids, latent), F32), table, dst_pick, src_pick_t, slope, enc_src_w,
        far=(3,), scratch=(edge_buf(edges, BF16), sem(1)),
    )
    grad_grid = call(join_kernel, shape((grids, latent), BF16), own_grad, swap(mate_grad))
    return (mesh_out, grad_grid, grad_mesh)


def solution(mesh):
    shard = ("band", "feat")
    placed = (P(shard, None), P(shard, None), P(shard), P(shard, None), P(shard), P(shard), P(shard))
    placed += (P(),) * 10 + (P(shard, None),)
    return jax.shard_map(
        per_device,
        mesh=mesh,
        in_specs=placed,
        out_specs=(P(shard, None), P(shard, None), P(shard, None)),
        check_vma=False,
    )
```

```python
import jax
import jax.numpy as jnp
from jax import lax
from jax.experimental import pallas as pl
from jax.experimental.pallas import tpu as pltpu
from jax.sharding import PartitionSpec as P

BF16 = jnp.bfloat16
F32 = jnp.float32


def dot(left, right):
    return jnp.dot(left, right, preferred_element_type=F32)


def dot_t(left, right):
    return lax.dot_general(left, right, (((1,), (1,)), ((), ())), preferred_element_type=F32)


def split(values):
    high = values.astype(BF16)
    return high, (values - high.astype(F32)).astype(BF16)


def wide_dot(values, weight, product):
    rows = values.shape[0]
    high, low = split(values)
    both = product(jnp.concatenate([high.astype(F32), low.astype(F32)], axis=0).astype(BF16), weight)
    return both[:rows] + both[rows:]


def layer_norm(values, gain):
    average = jnp.mean(values, axis=-1, keepdims=True)
    centred = values - average
    spread = jnp.mean(centred * centred, axis=-1, keepdims=True)
    inv_std = lax.rsqrt(spread + 1e-05)
    normed = centred * inv_std
    return normed * gain, normed, inv_std


def norm_back(normed, inv_std, gain, upstream):
    scaled = upstream * gain
    return inv_std * (
        scaled
        - jnp.mean(scaled, axis=-1, keepdims=True)
        - normed * jnp.mean(scaled * normed, axis=-1, keepdims=True)
    )


def call(body, out, *args, far=(), far_out=(), small=(), scratch=(), limit=16, cost=1):
    place = lambda there: pl.BlockSpec(memory_space=pltpu.HBM if there else pltpu.VMEM)
    single = not isinstance(out, tuple)
    outs = (out,) if single else out
    out_specs = tuple(place(i in far_out) for i in range(len(outs)))
    outs = tuple(
        pltpu.HBM(one.shape, one.dtype) if i in far_out else one for i, one in enumerate(outs)
    )
    args = tuple(
        pltpu.with_memory_space_constraint(arg, pltpu.HBM) if i in far else arg
        for i, arg in enumerate(args)
    )
    return pl.pallas_call(
        body,
        out_shape=outs[0] if single else outs,
        in_specs=[
            pl.BlockSpec(memory_space=pltpu.SMEM) if i in small else place(i in far)
            for i in range(len(args))
        ],
        out_specs=out_specs[0] if single else out_specs,
        scratch_shapes=scratch,
        compiler_params=pltpu.CompilerParams(vmem_limit_bytes=limit * 2**20 or None),
        cost_estimate=pl.CostEstimate(
            flops=cost * 4 * 10**9, bytes_accessed=cost * 2**22, transcendentals=0
        ),
    )(*args)


def dot_first(left, right):
    return lax.dot_general(left, right, (((0,), (0,)), ((), ())), preferred_element_type=F32)


def row_copies(source, target, sems, tile, offset=0):
    return [
        pltpu.make_async_copy(
            source.at[offset + i * tile : offset + (i + 1) * tile, :],
            target.at[i * tile : (i + 1) * tile, :],
            sems.at[i],
        )
        for i in range(sems.shape[0])
    ]


def silu_parts(values):
    sigma = 0.5 + 0.5 * jnp.tanh(0.5 * values)
    hidden = values * sigma
    return hidden.astype(BF16), sigma * (1.0 + (values - hidden))


def tile_kernel(mesh_ref, tiled_ref, buf, sem):
    copy = pltpu.make_async_copy(mesh_ref, buf, sem.at[0])
    copy.start()
    copy.wait()
    times = tiled_ref.shape[0] // buf.shape[0]
    tiled_ref[...] = jnp.concatenate([buf[...].astype(F32)] * times, axis=0).astype(BF16)


def prep_kernel(
    grid_ref, cotangent_ref, src_ref, peer_ref, slot_ref, sender_ref, receiver_ref,
    pack_ref, near_ref, cotangent_buf, index_buf, near_buf, sems,
):
    count, latent = cotangent_buf.shape
    grids = grid_ref.shape[0]
    half = sender_ref.shape[1]
    pairs = (
        (src_ref, index_buf.at[0]),
        (peer_ref, index_buf.at[1]),
        (slot_ref, index_buf.at[2]),
        (sender_ref, near_buf.at[:, :half]),
        (receiver_ref, near_buf.at[:, half:]),
        (cotangent_ref, cotangent_buf),
        (grid_ref, pack_ref.at[:grids, :]),
    )
    copies = [pltpu.make_async_copy(*pair, sems.at[i]) for i, pair in enumerate(pairs)]
    for copy in copies:
        copy.start()
    for copy in copies[:6]:
        copy.wait()
    spare = pack_ref.shape[0] - grids
    place = lax.broadcasted_iota(jnp.int32, (spare, latent), 0)
    index = jnp.where(place == 0, index_buf[0], jnp.where(place == 1, index_buf[1], index_buf[2]))
    pack_ref[grids:, :] = index.astype(F32).astype(BF16)
    ends = jnp.broadcast_to(near_buf[...], (count, 2 * half)).astype(F32)
    near_ref[...] = jnp.concatenate([cotangent_buf[...].astype(F32), ends], axis=0).astype(BF16)
    copies[6].wait()


def src_kernel(own_ref, mate_ref, pick_ref, rows_ref):
    tile = own_ref.shape[0]
    edges = pick_ref.shape[0]
    for start in range(0, edges, tile):
        grid_ref = own_ref if start < edges // 2 else mate_ref
        picked = dot(pick_ref[start : start + tile, :], grid_ref[:tile, :])
        rows_ref[start : start + tile, :] = picked.astype(BF16)


def stack_split(values):
    high = values.astype(BF16).astype(F32)
    return jnp.concatenate([high, values - high], axis=0).astype(BF16)


def spread_rows(pick, table):
    half = table.shape[0] // 2
    return dot(pick, table[:half]) + dot(pick, table[half:])


def enc_kernel(
    rows_ref, dst_ref, dst_t_ref, mesh_ref, src_w_ref, dst_w_ref, bias_ref, sum_ref, slope_ref,
    both, slope_buf, sems,
):
    latent = dst_w_ref.shape[1]
    tile = slope_buf.shape[0] // sems.shape[0]
    leaving = row_copies(slope_buf, slope_ref, sems, tile)
    table = stack_split(dot(mesh_ref[...], dst_w_ref[...]) + bias_ref[...])
    for i, copy in enumerate(leaving):
        rows = slice(i * tile, (i + 1) * tile)
        spread = spread_rows(dst_ref[rows, :], table)
        hidden, slope = silu_parts(dot(rows_ref[rows, :], src_w_ref[...]) + spread)
        both[rows, :latent] = hidden
        both[rows, latent:] = slope.astype(BF16)
        slope_buf[rows, :] = slope.astype(BF16)
        copy.start()
    total = dot(dst_t_ref[...], both[...])
    nodes = sum_ref.shape[1] // 2
    chunked = lambda v: v.reshape(-1, nodes, latent)
    sum_ref[...] = jnp.concatenate(
        [chunked(total[:, :latent]), chunked(total[:, latent:])], axis=1
    ).astype(BF16)
    for copy in leaving:
        copy.wait()


def mid_kernel(
    parts_ref, weight_ref, gain_ref, mesh_ref, near_ref, packet_ref, agg_ref, slopes_ref
):
    count = mesh_ref.shape[0]
    summed = jnp.sum(parts_ref[...].astype(F32), axis=0)
    agg = wide_dot(summed[:count], weight_ref[...], dot)
    slopes_ref[...] = summed[count:]
    agg_ref[...] = agg
    mid = mesh_ref[...].astype(F32) + layer_norm(agg, gain_ref[...])[0]
    packet_ref[...] = jnp.concatenate([mid, near_ref[...].astype(F32)], axis=0).astype(BF16)


def edge_ends(index, info_ref, offset, inside, group, count):
    half = index.shape[1] // 2
    source, receiver = index[:, :half], index[:, half:]
    bits = count.bit_length() - 1
    shift = offset + jnp.right_shift(source, bits) - 1
    one, two = info_ref[0], info_ref[1]
    spot = jnp.where(
        shift == 0, 4,
        jnp.where(
            shift == one, 0, jnp.where(shift == -one, 1, jnp.where(shift == two, 2, 3))
        ),
    )
    keep = lambda column: column * inside + (inside - 1)
    return (
        keep(spot * count + jnp.bitwise_and(source, count - 1)),
        keep((5 + group) * count + receiver),
    )


def proc_kernel(
    halo_ref, own_ref, info_ref, src_w_ref, dst_w_ref, out_w_ref,
    bias_ref, gain_ref, enc_agg_ref, enc_gain_ref, out_ref, grad_ref, tiled_ref,
):
    count = out_ref.shape[0]
    own = own_ref[...].astype(F32)
    halo = halo_ref[...].astype(F32)
    size = own.shape[0]
    met = [
        jnp.where(info_ref[4] == 0, halo[start : start + size], halo[start + size : start + 2 * size])
        for start in range(0, 8 * size, 2 * size)
    ]
    packets = [met[0], met[1], own]
    one, two, mid = (packet[:count] for packet in packets)
    upstreams = jnp.concatenate([packet[count : 2 * count] for packet in packets], axis=0)
    index = [packet[2 * count : 2 * count + 1].astype(jnp.int32) for packet in packets]
    step = info_ref[0]
    columns = [
        edge_ends(index[0], info_ref, step, info_ref[2], 0, count),
        edge_ends(index[1], info_ref, -step, info_ref[3], 1, count),
        edge_ends(index[2], info_ref, 0, 1, 2, count),
    ]
    sender, receiver = (jnp.concatenate(column, axis=1) for column in zip(*columns))
    ids = lax.broadcasted_iota(jnp.int32, (8 * count, sender.shape[1]), 0)
    chosen = jnp.where(jnp.logical_or(ids == sender, ids == receiver), 1.0, 0.0)
    pick_t = chosen.astype(BF16)
    pick = jnp.concatenate([chosen] * 2, axis=0).astype(BF16)

    rows = [one, two, met[2][:count], met[3][:count], mid]
    senders = jnp.concatenate(rows, axis=0).astype(BF16)
    receivers = jnp.concatenate([one, two, mid], axis=0).astype(BF16)
    table = jnp.concatenate(
        [dot(senders, src_w_ref[...]), dot(receivers, dst_w_ref[...]) + bias_ref[...]], axis=0
    )
    hidden, slope = silu_parts(dot_first(pick, stack_split(table)))
    summed = dot(pick_t, hidden)[5 * count :]
    agg = wide_dot(summed, out_w_ref[...], dot)
    shifted, normed, inv_std = layer_norm(agg, gain_ref[...])
    out_ref[...] = (mid + shifted[2 * count :]).astype(BF16)
    grad_agg = norm_back(normed, inv_std, gain_ref[...], upstreams).astype(BF16)
    back = dot_t(grad_agg, out_w_ref[...])
    blank = jnp.zeros((5 * count, back.shape[1]), F32)
    spread = dot_first(pick, stack_split(jnp.concatenate([blank, back], axis=0)))
    sums = dot(pick_t, (spread * slope).astype(BF16))
    sender_sum = wide_dot(sums[4 * count : 5 * count], src_w_ref[...], dot_t)
    receiver_sum = wide_dot(sums[7 * count :], dst_w_ref[...], dot_t)
    grad = upstreams[2 * count :] + receiver_sum + sender_sum
    grad_ref[...] = grad
    _, normed, inv_std = layer_norm(enc_agg_ref[...], enc_gain_ref[...])
    rows = norm_back(normed, inv_std, enc_gain_ref[...], grad)
    times = tiled_ref.shape[0] // count
    tiled_ref[...] = jnp.concatenate([rows] * times, axis=0).astype(BF16)


def mesh_kernel(tiled_ref, slopes_ref, grad_ref, out_w_ref, dst_w_ref, out_ref):
    count = grad_ref.shape[0]
    rows = dot_t(tiled_ref[: 2 * count, :], out_w_ref[...])[:count]
    out_ref[...] = (
        grad_ref[...] + wide_dot(rows * slopes_ref[...], dst_w_ref[...], dot_t)
    ).astype(BF16)


def mate_kernel(
    grad_ref, dst_ref, pick_t_ref, slope_ref, out_w_ref, src_w_ref, table_ref, part_ref, buf, sems
):
    half = dst_ref.shape[0] // 2
    (arriving,) = row_copies(slope_ref, buf, sems, half, half)
    arriving.start()
    table = stack_split(dot_t(grad_ref[...], out_w_ref[...]))
    table_ref[...] = table
    spread = spread_rows(dst_ref[half:, :], table)
    arriving.wait()
    edge = (spread * buf[...].astype(F32)).astype(BF16)
    part_ref[...] = wide_dot(dot(pick_t_ref[:, half:], edge), src_w_ref[...], dot_t).astype(BF16)


def own_kernel(table_ref, dst_ref, pick_t_ref, slope_ref, src_w_ref, part_ref, buf, sems):
    half = dst_ref.shape[0] // 2
    (arriving,) = row_copies(slope_ref, buf, sems, half)
    arriving.start()
    spread = spread_rows(dst_ref[:half, :], table_ref[...])
    arriving.wait()
    edge = (spread * buf[...].astype(F32)).astype(BF16)
    part_ref[...] = wide_dot(dot(pick_t_ref[:, :half], edge), src_w_ref[...], dot_t)


def join_kernel(own_ref, mate_ref, out_ref):
    out_ref[...] = (own_ref[...] + mate_ref[...].astype(F32)).astype(BF16)


def per_device(
    grid_latent,
    mesh_latent,
    g2m_src,
    g2m_peer,
    g2m_slot,
    proc_src,
    proc_dst,
    enc_src_w,
    enc_dst_w,
    enc_out_w,
    enc_bias,
    enc_gain,
    proc_src_w,
    proc_dst_w,
    proc_out_w,
    proc_bias,
    proc_gain,
    cotangent,
):
    feats = lax.axis_size("feat")
    bands = lax.axis_size("band")
    chips = feats // 2
    core = lax.axis_index("feat") % 2
    band = lax.axis_index("band")
    edges = g2m_src.shape[0]
    grids, latent = grid_latent.shape
    nodes = mesh_latent.shape[0]
    plane_nodes = chips * nodes
    plane = [[2 * chip + side for chip in range(chips)] for side in range(2)]
    shape = jax.ShapeDtypeStruct
    row = lambda vector: vector.reshape(1, latent)
    sem = lambda count: pltpu.SemaphoreType.DMA((count,))
    edge_buf = lambda count, kind: pltpu.VMEM((count, latent), kind)

    def exchange(values):
        return lax.all_to_all(
            values.reshape(chips, -1, latent), "feat", split_axis=0, concat_axis=0, tiled=True,
            axis_index_groups=plane,
        )

    def swap(values):
        return lax.ppermute(values, "feat", [(i, i ^ 1) for i in range(feats)])

    near_side = lambda step: [(i, i ^ step) for i in range(bands)]
    far_side = lambda step: [
        pair
        for i in range(bands - step)
        if i & step
        for pair in ((i, i + step), (i + step, i))
    ]

    def meet(values, *sides):
        pairs = [
            (source * feats + feat, target * feats + feat)
            for feat in range(feats)
            for source, target in sides[feat % 2]
        ]
        return lax.ppermute(values, ("band", "feat"), pairs)

    def both_cores(values):
        return lax.all_gather(
            values, "feat", axis=0, tiled=True,
            axis_index_groups=[[i, i + 1] for i in range(0, feats, 2)],
        )

    line = lambda index: index.reshape(1, edges)

    tiled_mesh = call(
        tile_kernel, shape((plane_nodes, latent), BF16), mesh_latent,
        far=(0,), scratch=(edge_buf(nodes, BF16), sem(1)),
    )
    pack, near = call(
        prep_kernel,
        (shape((grids + 16, latent), BF16), shape((2 * nodes, latent), BF16)),
        grid_latent, cotangent, line(g2m_src), line(g2m_peer), line(g2m_slot),
        proc_src.reshape(1, -1), proc_dst.reshape(1, -1),
        far=range(7), cost=0,
        scratch=(
            edge_buf(nodes, BF16),
            pltpu.VMEM((3, 1, edges), jnp.int32),
            pltpu.VMEM((1, latent), jnp.int32),
            sem(7),
        ),
    )
    packs = both_cores(pack)
    mate_pack = lax.dynamic_slice_in_dim(packs, (1 - core) * pack.shape[0], pack.shape[0])
    mesh_all = exchange(tiled_mesh).reshape(plane_nodes, latent)

    mate_index = mate_pack[grids : grids + 3].astype(jnp.int32)
    joined = lambda own, place: jnp.concatenate([own, mate_index[place]])
    source, peer, slot = joined(g2m_src, 0), joined(g2m_peer[:, 0], 1), joined(g2m_slot, 2)
    target = jnp.where(peer % 2 == core, peer // 2 * nodes + slot, -1)
    grid_ids = jnp.arange(grids, dtype=jnp.int32)
    node_ids = jnp.arange(plane_nodes, dtype=jnp.int32)
    src_pick = (source[:, None] == grid_ids[None, :]).astype(BF16)
    src_pick_t = (source[None, :] == grid_ids[:, None]).astype(BF16)
    dst_pick = (target[:, None] == node_ids[None, :]).astype(BF16)
    dst_pick_t = (target[None, :] == node_ids[:, None]).astype(BF16)

    step_one = jnp.where(band & 1 == 0, 1, -1)
    step_two = jnp.where(band & 2 == 0, 2, -2)
    inside = lambda place: jnp.logical_and(place >= 0, place < bands)
    info = jnp.stack([step_one, step_two, inside(band + step_one), inside(band - step_one), core])

    src_rows = call(
        src_kernel, shape((2 * edges, latent), BF16), grid_latent, mate_pack, src_pick, cost=0,
    )
    partial, slope = call(
        enc_kernel,
        (shape((chips, 2 * nodes, latent), BF16), shape((2 * edges, latent), BF16)),
        src_rows, dst_pick, dst_pick_t, mesh_all, enc_src_w, enc_dst_w, row(enc_bias),
        far_out=(1,),
        scratch=(pltpu.VMEM((2 * edges, 2 * latent), BF16), edge_buf(2 * edges, BF16), sem(4)),
    )
    packet, enc_agg, slopes = call(
        mid_kernel,
        (
            shape((3 * nodes, latent), BF16),
            shape((nodes, latent), F32),
            shape((nodes, latent), F32),
        ),
        exchange(partial), enc_out_w, row(enc_gain), mesh_latent, near,
    )
    packets = both_cores(packet)
    halo = both_cores(
        jnp.concatenate(
            [
                meet(packets, near_side(1), near_side(2)),
                meet(packets, far_side(1), far_side(2)),
            ],
            axis=0,
        )
    )
    mesh_out, grad_mid, tiled = call(
        proc_kernel,
        (
            shape((nodes, latent), BF16),
            shape((nodes, latent), F32),
            shape((plane_nodes, latent), BF16),
        ),
        halo, packet, info.astype(jnp.int32), proc_src_w, proc_dst_w, proc_out_w, row(proc_bias),
        row(proc_gain), enc_agg, row(enc_gain),
        small=(2,),
    )
    grad_all = exchange(tiled).reshape(plane_nodes, latent)
    grad_mesh = call(
        mesh_kernel, shape((nodes, latent), BF16), tiled, slopes, grad_mid, enc_out_w, enc_dst_w,
    )
    table, mate_grad = call(
        mate_kernel, (shape((2 * plane_nodes, latent), BF16), shape((grids, latent), BF16)),
        grad_all, dst_pick, src_pick_t, slope, enc_out_w, enc_src_w,
        far=(3,), scratch=(edge_buf(edges, BF16), sem(1)),
    )
    own_grad = call(
        own_kernel, shape((grids, latent), F32), table, dst_pick, src_pick_t, slope, enc_src_w,
        far=(3,), scratch=(edge_buf(edges, BF16), sem(1)),
    )
    grad_grid = call(join_kernel, shape((grids, latent), BF16), own_grad, swap(mate_grad))
    return (mesh_out, grad_grid, grad_mesh)


def solution(mesh):
    shard = ("band", "feat")
    placed = (P(shard, None), P(shard, None), P(shard), P(shard, None), P(shard), P(shard), P(shard))
    placed += (P(),) * 10 + (P(shard, None),)
    return jax.shard_map(
        per_device,
        mesh=mesh,
        in_specs=placed,
        out_specs=(P(shard, None), P(shard, None), P(shard, None)),
        check_vma=False,
    )
```

```python
import jax
import jax.numpy as jnp
from jax import lax
from jax.experimental import pallas as pl
from jax.experimental.pallas import tpu as pltpu
from jax.sharding import PartitionSpec as P

BF16 = jnp.bfloat16
F32 = jnp.float32


def dot(left, right):
    return jnp.dot(left, right, preferred_element_type=F32)


def dot_t(left, right):
    return lax.dot_general(left, right, (((1,), (1,)), ((), ())), preferred_element_type=F32)


def split(values):
    high = values.astype(BF16)
    return high, (values - high.astype(F32)).astype(BF16)


def wide_dot(values, weight, product):
    rows = values.shape[0]
    high, low = split(values)
    both = product(jnp.concatenate([high.astype(F32), low.astype(F32)], axis=0).astype(BF16), weight)
    return both[:rows] + both[rows:]


def layer_norm(values, gain):
    average = jnp.mean(values, axis=-1, keepdims=True)
    centred = values - average
    spread = jnp.mean(centred * centred, axis=-1, keepdims=True)
    inv_std = lax.rsqrt(spread + 1e-05)
    normed = centred * inv_std
    return normed * gain, normed, inv_std


def norm_back(normed, inv_std, gain, upstream):
    scaled = upstream * gain
    return inv_std * (
        scaled
        - jnp.mean(scaled, axis=-1, keepdims=True)
        - normed * jnp.mean(scaled * normed, axis=-1, keepdims=True)
    )


def call(body, out, *args, far=(), far_out=(), small=(), scratch=(), limit=16, cost=1):
    place = lambda there: pl.BlockSpec(memory_space=pltpu.HBM if there else pltpu.VMEM)
    single = not isinstance(out, tuple)
    outs = (out,) if single else out
    out_specs = tuple(place(i in far_out) for i in range(len(outs)))
    outs = tuple(
        pltpu.HBM(one.shape, one.dtype) if i in far_out else one for i, one in enumerate(outs)
    )
    args = tuple(
        pltpu.with_memory_space_constraint(arg, pltpu.HBM) if i in far else arg
        for i, arg in enumerate(args)
    )
    return pl.pallas_call(
        body,
        out_shape=outs[0] if single else outs,
        in_specs=[
            pl.BlockSpec(memory_space=pltpu.SMEM) if i in small else place(i in far)
            for i in range(len(args))
        ],
        out_specs=out_specs[0] if single else out_specs,
        scratch_shapes=scratch,
        compiler_params=pltpu.CompilerParams(vmem_limit_bytes=limit * 2**20 or None),
        cost_estimate=pl.CostEstimate(
            flops=cost * 4 * 10**9, bytes_accessed=cost * 2**22, transcendentals=0
        ),
    )(*args)


def dot_first(left, right):
    return lax.dot_general(left, right, (((0,), (0,)), ((), ())), preferred_element_type=F32)


def row_copies(source, target, sems, tile, offset=0):
    return [
        pltpu.make_async_copy(
            source.at[offset + i * tile : offset + (i + 1) * tile, :],
            target.at[i * tile : (i + 1) * tile, :],
            sems.at[i],
        )
        for i in range(sems.shape[0])
    ]


def silu_parts(values):
    sigma = 0.5 + 0.5 * jnp.tanh(0.5 * values)
    hidden = values * sigma
    return hidden.astype(BF16), sigma * (1.0 + (values - hidden))


def tile_kernel(mesh_ref, tiled_ref, buf, sem):
    copy = pltpu.make_async_copy(mesh_ref, buf, sem.at[0])
    copy.start()
    copy.wait()
    times = tiled_ref.shape[0] // buf.shape[0]
    tiled_ref[...] = jnp.concatenate([buf[...].astype(F32)] * times, axis=0).astype(BF16)


def prep_kernel(
    grid_ref, cotangent_ref, src_ref, peer_ref, slot_ref, sender_ref, receiver_ref,
    pack_ref, near_ref, cotangent_buf, index_buf, near_buf, sems,
):
    count, latent = cotangent_buf.shape
    grids = grid_ref.shape[0]
    half = sender_ref.shape[1]
    pairs = (
        (src_ref, index_buf.at[0]),
        (peer_ref, index_buf.at[1]),
        (slot_ref, index_buf.at[2]),
        (sender_ref, near_buf.at[:, :half]),
        (receiver_ref, near_buf.at[:, half:]),
        (cotangent_ref, cotangent_buf),
        (grid_ref, pack_ref.at[:grids, :]),
    )
    copies = [pltpu.make_async_copy(*pair, sems.at[i]) for i, pair in enumerate(pairs)]
    for copy in copies:
        copy.start()
    for copy in copies[:6]:
        copy.wait()
    spare = pack_ref.shape[0] - grids
    place = lax.broadcasted_iota(jnp.int32, (spare, latent), 0)
    index = jnp.where(place == 0, index_buf[0], jnp.where(place == 1, index_buf[1], index_buf[2]))
    pack_ref[grids:, :] = index.astype(F32).astype(BF16)
    ends = jnp.broadcast_to(near_buf[...], (count, 2 * half)).astype(F32)
    near_ref[...] = jnp.concatenate([cotangent_buf[...].astype(F32), ends], axis=0).astype(BF16)
    copies[6].wait()


def src_kernel(own_ref, mate_ref, pick_ref, rows_ref):
    tile = own_ref.shape[0]
    edges = pick_ref.shape[0]
    for start in range(0, edges, tile):
        grid_ref = own_ref if start < edges // 2 else mate_ref
        picked = dot(pick_ref[start : start + tile, :], grid_ref[:tile, :])
        rows_ref[start : start + tile, :] = picked.astype(BF16)


def stack_split(values):
    high = values.astype(BF16).astype(F32)
    return jnp.concatenate([high, values - high], axis=0).astype(BF16)


def spread_rows(pick, table):
    half = table.shape[0] // 2
    return dot(pick, table[:half]) + dot(pick, table[half:])


def enc_kernel(
    rows_ref, dst_ref, dst_t_ref, mesh_ref, src_w_ref, dst_w_ref, bias_ref, sum_ref, slope_ref,
    both, slope_buf, sems,
):
    latent = dst_w_ref.shape[1]
    tile = slope_buf.shape[0] // sems.shape[0]
    leaving = row_copies(slope_buf, slope_ref, sems, tile)
    table = stack_split(dot(mesh_ref[...], dst_w_ref[...]) + bias_ref[...])
    for i, copy in enumerate(leaving):
        rows = slice(i * tile, (i + 1) * tile)
        spread = spread_rows(dst_ref[rows, :], table)
        hidden, slope = silu_parts(dot(rows_ref[rows, :], src_w_ref[...]) + spread)
        both[rows, :latent] = hidden
        both[rows, latent:] = slope.astype(BF16)
        slope_buf[rows, :] = slope.astype(BF16)
        copy.start()
    total = dot(dst_t_ref[...], both[...])
    nodes = sum_ref.shape[1] // 2
    chunked = lambda v: v.reshape(-1, nodes, latent)
    sum_ref[...] = jnp.concatenate(
        [chunked(total[:, :latent]), chunked(total[:, latent:])], axis=1
    ).astype(BF16)
    for copy in leaving:
        copy.wait()


def mid_kernel(
    parts_ref, weight_ref, gain_ref, mesh_ref, near_ref, packet_ref, agg_ref, slopes_ref
):
    count = mesh_ref.shape[0]
    summed = jnp.sum(parts_ref[...].astype(F32), axis=0)
    agg = wide_dot(summed[:count], weight_ref[...], dot)
    slopes_ref[...] = summed[count:]
    agg_ref[...] = agg
    mid = mesh_ref[...].astype(F32) + layer_norm(agg, gain_ref[...])[0]
    packet_ref[...] = jnp.concatenate([mid, near_ref[...].astype(F32)], axis=0).astype(BF16)


def edge_ends(index, info_ref, offset, inside, group, count):
    half = index.shape[1] // 2
    source, receiver = index[:, :half], index[:, half:]
    bits = count.bit_length() - 1
    shift = offset + jnp.right_shift(source, bits) - 1
    one, two = info_ref[0], info_ref[1]
    spot = jnp.where(
        shift == 0, 4,
        jnp.where(
            shift == one, 0, jnp.where(shift == -one, 1, jnp.where(shift == two, 2, 3))
        ),
    )
    keep = lambda column: column * inside + (inside - 1)
    return (
        keep(spot * count + jnp.bitwise_and(source, count - 1)),
        keep((5 + group) * count + receiver),
    )


def proc_kernel(
    halo_ref, own_ref, info_ref, src_w_ref, dst_w_ref, out_w_ref,
    bias_ref, gain_ref, enc_agg_ref, enc_gain_ref, out_ref, grad_ref, tiled_ref,
):
    count = out_ref.shape[0]
    own = own_ref[...].astype(F32)
    halo = halo_ref[...].astype(F32)
    size = own.shape[0]
    met = [
        jnp.where(info_ref[4] == 0, halo[start : start + size], halo[start + size : start + 2 * size])
        for start in range(0, 8 * size, 2 * size)
    ]
    packets = [met[0], met[1], own]
    one, two, mid = (packet[:count] for packet in packets)
    upstreams = jnp.concatenate([packet[count : 2 * count] for packet in packets], axis=0)
    index = [packet[2 * count : 2 * count + 1].astype(jnp.int32) for packet in packets]
    step = info_ref[0]
    columns = [
        edge_ends(index[0], info_ref, step, info_ref[2], 0, count),
        edge_ends(index[1], info_ref, -step, info_ref[3], 1, count),
        edge_ends(index[2], info_ref, 0, 1, 2, count),
    ]
    sender, receiver = (jnp.concatenate(column, axis=1) for column in zip(*columns))
    ids = lax.broadcasted_iota(jnp.int32, (8 * count, sender.shape[1]), 0)
    chosen = jnp.where(jnp.logical_or(ids == sender, ids == receiver), 1.0, 0.0)
    pick_t = chosen.astype(BF16)
    pick = jnp.concatenate([chosen] * 2, axis=0).astype(BF16)

    rows = [one, two, met[2][:count], met[3][:count], mid]
    senders = jnp.concatenate(rows, axis=0).astype(BF16)
    receivers = jnp.concatenate([one, two, mid], axis=0).astype(BF16)
    table = jnp.concatenate(
        [dot(senders, src_w_ref[...]), dot(receivers, dst_w_ref[...]) + bias_ref[...]], axis=0
    )
    hidden, slope = silu_parts(dot_first(pick, stack_split(table)))
    summed = dot(pick_t, hidden)[5 * count :]
    agg = wide_dot(summed, out_w_ref[...], dot)
    shifted, normed, inv_std = layer_norm(agg, gain_ref[...])
    out_ref[...] = (mid + shifted[2 * count :]).astype(BF16)
    grad_agg = norm_back(normed, inv_std, gain_ref[...], upstreams).astype(BF16)
    back = dot_t(grad_agg, out_w_ref[...])
    blank = jnp.zeros((5 * count, back.shape[1]), F32)
    spread = dot_first(pick, stack_split(jnp.concatenate([blank, back], axis=0)))
    sums = dot(pick_t, (spread * slope).astype(BF16))
    sender_sum = wide_dot(sums[4 * count : 5 * count], src_w_ref[...], dot_t)
    receiver_sum = wide_dot(sums[7 * count :], dst_w_ref[...], dot_t)
    grad = upstreams[2 * count :] + receiver_sum + sender_sum
    grad_ref[...] = grad
    _, normed, inv_std = layer_norm(enc_agg_ref[...], enc_gain_ref[...])
    rows = norm_back(normed, inv_std, enc_gain_ref[...], grad)
    times = tiled_ref.shape[0] // count
    tiled_ref[...] = jnp.concatenate([rows] * times, axis=0).astype(BF16)


def mesh_kernel(tiled_ref, slopes_ref, grad_ref, out_w_ref, dst_w_ref, out_ref):
    count = grad_ref.shape[0]
    rows = dot_t(tiled_ref[: 2 * count, :], out_w_ref[...])[:count]
    out_ref[...] = (
        grad_ref[...] + wide_dot(rows * slopes_ref[...], dst_w_ref[...], dot_t)
    ).astype(BF16)


def mate_kernel(
    grad_ref, dst_ref, pick_t_ref, slope_ref, out_w_ref, src_w_ref, table_ref, part_ref, buf, sems
):
    half = dst_ref.shape[0] // 2
    (arriving,) = row_copies(slope_ref, buf, sems, half, half)
    arriving.start()
    table = stack_split(dot_t(grad_ref[...], out_w_ref[...]))
    table_ref[...] = table
    spread = spread_rows(dst_ref[half:, :], table)
    arriving.wait()
    edge = (spread * buf[...].astype(F32)).astype(BF16)
    part_ref[...] = wide_dot(dot(pick_t_ref[:, half:], edge), src_w_ref[...], dot_t).astype(BF16)


def own_kernel(table_ref, dst_ref, pick_t_ref, slope_ref, src_w_ref, part_ref, buf, sems):
    half = dst_ref.shape[0] // 2
    (arriving,) = row_copies(slope_ref, buf, sems, half)
    arriving.start()
    spread = spread_rows(dst_ref[:half, :], table_ref[...])
    arriving.wait()
    edge = (spread * buf[...].astype(F32)).astype(BF16)
    part_ref[...] = wide_dot(dot(pick_t_ref[:, :half], edge), src_w_ref[...], dot_t)


def join_kernel(own_ref, mate_ref, out_ref):
    out_ref[...] = (own_ref[...] + mate_ref[...].astype(F32)).astype(BF16)


def per_device(
    grid_latent,
    mesh_latent,
    g2m_src,
    g2m_peer,
    g2m_slot,
    proc_src,
    proc_dst,
    enc_src_w,
    enc_dst_w,
    enc_out_w,
    enc_bias,
    enc_gain,
    proc_src_w,
    proc_dst_w,
    proc_out_w,
    proc_bias,
    proc_gain,
    cotangent,
):
    feats = lax.axis_size("feat")
    bands = lax.axis_size("band")
    chips = feats // 2
    core = lax.axis_index("feat") % 2
    band = lax.axis_index("band")
    edges = g2m_src.shape[0]
    grids, latent = grid_latent.shape
    nodes = mesh_latent.shape[0]
    plane_nodes = chips * nodes
    plane = [[2 * chip + side for chip in range(chips)] for side in range(2)]
    shape = jax.ShapeDtypeStruct
    row = lambda vector: vector.reshape(1, latent)
    sem = lambda count: pltpu.SemaphoreType.DMA((count,))
    edge_buf = lambda count, kind: pltpu.VMEM((count, latent), kind)

    def exchange(values):
        return lax.all_to_all(
            values.reshape(chips, -1, latent), "feat", split_axis=0, concat_axis=0, tiled=True,
            axis_index_groups=plane,
        )

    def swap(values):
        return lax.ppermute(values, "feat", [(i, i ^ 1) for i in range(feats)])

    near_side = lambda step: [(i, i ^ step) for i in range(bands)]
    far_side = lambda step: [
        pair
        for i in range(bands - step)
        if i & step
        for pair in ((i, i + step), (i + step, i))
    ]

    def meet(values, *sides):
        pairs = [
            (source * feats + feat, target * feats + feat)
            for feat in range(feats)
            for source, target in sides[feat % 2]
        ]
        return lax.ppermute(values, ("band", "feat"), pairs)

    def both_cores(values):
        return lax.all_gather(
            values, "feat", axis=0, tiled=True,
            axis_index_groups=[[i, i + 1] for i in range(0, feats, 2)],
        )

    line = lambda index: index.reshape(1, edges)

    tiled_mesh = call(
        tile_kernel, shape((plane_nodes, latent), BF16), mesh_latent,
        far=(0,), scratch=(edge_buf(nodes, BF16), sem(1)),
    )
    pack, near = call(
        prep_kernel,
        (shape((grids + 16, latent), BF16), shape((2 * nodes, latent), BF16)),
        grid_latent, cotangent, line(g2m_src), line(g2m_peer), line(g2m_slot),
        proc_src.reshape(1, -1), proc_dst.reshape(1, -1),
        far=range(7), cost=0,
        scratch=(
            edge_buf(nodes, BF16),
            pltpu.VMEM((3, 1, edges), jnp.int32),
            pltpu.VMEM((1, latent), jnp.int32),
            sem(7),
        ),
    )
    packs = both_cores(pack)
    mate_pack = lax.dynamic_slice_in_dim(packs, (1 - core) * pack.shape[0], pack.shape[0])
    mesh_all = exchange(tiled_mesh).reshape(plane_nodes, latent)

    mate_index = mate_pack[grids : grids + 3].astype(jnp.int32)
    joined = lambda own, place: jnp.concatenate([own, mate_index[place]])
    source, peer, slot = joined(g2m_src, 0), joined(g2m_peer[:, 0], 1), joined(g2m_slot, 2)
    target = jnp.where(peer % 2 == core, peer // 2 * nodes + slot, -1)
    grid_ids = jnp.arange(grids, dtype=jnp.int32)
    node_ids = jnp.arange(plane_nodes, dtype=jnp.int32)
    src_pick = (source[:, None] == grid_ids[None, :]).astype(BF16)
    src_pick_t = (source[None, :] == grid_ids[:, None]).astype(BF16)
    dst_pick = (target[:, None] == node_ids[None, :]).astype(BF16)
    dst_pick_t = (target[None, :] == node_ids[:, None]).astype(BF16)

    step_one = jnp.where(band & 1 == 0, 1, -1)
    step_two = jnp.where(band & 2 == 0, 2, -2)
    inside = lambda place: jnp.logical_and(place >= 0, place < bands)
    info = jnp.stack([step_one, step_two, inside(band + step_one), inside(band - step_one), core])

    src_rows = call(
        src_kernel, shape((2 * edges, latent), BF16), grid_latent, mate_pack, src_pick,
    )
    partial, slope = call(
        enc_kernel,
        (shape((chips, 2 * nodes, latent), BF16), shape((2 * edges, latent), BF16)),
        src_rows, dst_pick, dst_pick_t, mesh_all, enc_src_w, enc_dst_w, row(enc_bias),
        far_out=(1,),
        scratch=(pltpu.VMEM((2 * edges, 2 * latent), BF16), edge_buf(2 * edges, BF16), sem(4)),
    )
    packet, enc_agg, slopes = call(
        mid_kernel,
        (
            shape((3 * nodes, latent), BF16),
            shape((nodes, latent), F32),
            shape((nodes, latent), F32),
        ),
        exchange(partial), enc_out_w, row(enc_gain), mesh_latent, near,
    )
    packets = both_cores(packet)
    halo = both_cores(
        jnp.concatenate(
            [
                meet(packets, near_side(1), near_side(2)),
                meet(packets, far_side(1), far_side(2)),
            ],
            axis=0,
        )
    )
    mesh_out, grad_mid, tiled = call(
        proc_kernel,
        (
            shape((nodes, latent), BF16),
            shape((nodes, latent), F32),
            shape((plane_nodes, latent), BF16),
        ),
        halo, packet, info.astype(jnp.int32), proc_src_w, proc_dst_w, proc_out_w, row(proc_bias),
        row(proc_gain), enc_agg, row(enc_gain),
        small=(2,),
    )
    grad_all = exchange(tiled).reshape(plane_nodes, latent)
    grad_mesh = call(
        mesh_kernel, shape((nodes, latent), BF16), tiled, slopes, grad_mid, enc_out_w, enc_dst_w,
    )
    table, mate_grad = call(
        mate_kernel, (shape((2 * plane_nodes, latent), BF16), shape((grids, latent), BF16)),
        grad_all, dst_pick, src_pick_t, slope, enc_out_w, enc_src_w,
        far=(3,), scratch=(edge_buf(edges, BF16), sem(1)),
    )
    own_grad = call(
        own_kernel, shape((grids, latent), F32), table, dst_pick, src_pick_t, slope, enc_src_w,
        far=(3,), scratch=(edge_buf(edges, BF16), sem(1)),
    )
    grad_grid = call(join_kernel, shape((grids, latent), BF16), own_grad, swap(mate_grad))
    return (mesh_out, grad_grid, grad_mesh)


def solution(mesh):
    shard = ("band", "feat")
    placed = (P(shard, None), P(shard, None), P(shard), P(shard, None), P(shard), P(shard), P(shard))
    placed += (P(),) * 10 + (P(shard, None),)
    return jax.shard_map(
        per_device,
        mesh=mesh,
        in_specs=placed,
        out_specs=(P(shard, None), P(shard, None), P(shard, None)),
        check_vma=False,
    )
```
